128 devices in a mesh: row: 8 (over z, core), col: 16 (over x, y).
Axes of the slice: x: 4, y: 4, z: 4, core: 2. Of those that a mesh axis runs over, the one named last changes fastest.
Arguments:
- node_codes: bfloat16 [262144, 768], P(('row', 'col')), may hold values from -127 to 127
- node_scales: bfloat16 [262144], P(('row', 'col')), may hold values from 0.0049743652 to 0.049804688
- target_rows: int32 [131072], P(('row', 'col')), may hold values from 0 to 2047
- owners: int32 [16384, 1], P(('row', 'col')), may hold values from 0 to 127; in each aligned block of 128 rows (0 to 127, 128 to 255, ...) at most 2 rows name the same one
- local_blocks: int32 [16384], P(('row', 'col')), may hold values from 0 to 63
- neighbours: int32 [131072, 10], P(('row', 'col')), may hold values from 0 to 4095
- weight_self: bfloat16 [768, 1024], replicated, may hold values from -0.21875 to 0.21875
- weight_neigh: bfloat16 [768, 1024], replicated, may hold values from -0.21875 to 0.21875
- bias: float32 [1024], replicated, may hold values from -3 to 3
- cotangent: bfloat16 [131072, 1024], P(('row', 'col')), may hold values from -0.016479492 to 0.016479492
Outputs:
- hidden: bfloat16 [131072, 1024], P(('row', 'col'))
- grad_self: float32 [768, 1024], replicated
- grad_neigh: float32 [768, 1024], replicated
- grad_bias: float32 [1024], replicated
The draws below stay inside these ranges and needn't reach their ends.
Inputs may be any that keep to these rules, and one draw needn't show every extreme that they name: `owners`: among the 128 requests of one device, at most 2 name the same owner, and some device's requests name one owner exactly 2 times.
All inputs are finite; a program needn't handle non-finite values.
Results may differ from the reference program's by a relative error of at most 0.013.
Values may be sent and summed in bfloat16 or wider, within the bound.
No kernel may reach another device: no remote copies, remote signals or barrier semaphores. Data moves between devices by JAX's collectives and lax.ppermute only.
A program may use at most 128 MiB of HBM per device.

```python
import math
import jax
import jax.numpy as jnp
import numpy as np
from jax import lax

F = 768
H = 1024
BR = 32
K = 10
CAP = 2
NODE_DEV = 2048
TGT = 1024
NB_DEV = 64
R_DEV = 128
NODES = 262144
TARGETS = 131072
REQS = 16384
N_ROW = 8
N_COL = 16


def touch_ends(result, key, low, high):
    longest = result.shape.index(max(result.shape))
    spots = []
    for shift in (0, 1):
        where = [jax.random.randint(jax.random.fold_in(key, axis), (), 0, length) for axis, length in enumerate(result.shape)]
        where[longest] = (where[longest] + shift) % result.shape[longest]
        spots.append(tuple(where))
    return result.at[spots[0]].set(low).at[spots[1]].set(high)


def block_levels(own_key, dims, shards, smallest, top_value):
    def one(dim, shards_of):
        steps = jax.random.uniform(jax.random.fold_in(jax.random.fold_in(own_key, 6), dim), (shards_of,), jnp.float32, smallest / len(shards), top_value / len(shards))
        return jnp.repeat(jnp.exp(steps), dims[dim] // shards_of).reshape((-1,) + (1,) * (len(dims) - dim - 1))

    factor_of = one(*shards[0])
    for cut in shards[1:]:
        factor_of = factor_of * one(*cut)
    return factor_of


def routed_block(rng, own, number, rows, count, top, bound, slope):
    ranking = jax.random.permutation(rng, count)
    crowded, usual = portions_of(count, rows * top, bound, slope, True), portions_of(count, rows * top, bound, slope, False)
    places = jnp.arange(count)

    def named(sizes, offset_by):
        used = int((sizes > 0).sum())
        fixed = max(1, used // 4)
        shifted = fixed + (places - fixed + offset_by * (used - fixed)) % max(1, count - fixed)
        return jnp.zeros((count,), jnp.int32).at[ranking[jnp.where(places < fixed, places, shifted)]].set(jnp.asarray(sizes, jnp.int32))

    sizes = jnp.where(number % 4 == 0, named(crowded, number // 4), named(usual, number - number // 4 - 1))
    mixed = jax.random.permutation(jax.random.fold_in(own, 3), count)
    donor, taker = mixed[0:count // 2 * 2:2], mixed[1:count // 2 * 2:2]
    slack = jnp.minimum(sizes[donor] - 1, bound - sizes[taker]) // 2
    slack = jnp.where((donor == ranking[0]) | (taker == ranking[0]) | (sizes[taker] == 0), 0, jnp.maximum(slack, 0))
    shifted = jax.random.randint(jax.random.fold_in(own, 4), (count // 2,), 0, 1 << 20) % (slack + 1)
    sizes = sizes.at[donor].add(-shifted).at[taker].add(shifted)
    items = jnp.searchsorted(jnp.cumsum(sizes), jnp.arange(rows * top), side="right").astype(jnp.int32)
    listing = items.reshape(top, rows).T
    listing = listing[jax.random.permutation(jax.random.fold_in(own, 1), rows)]
    offset_by = jax.random.randint(jax.random.fold_in(own, 2), (rows, 1), 0, top)
    return jnp.take_along_axis(listing, (jnp.arange(top)[None, :] + offset_by) % top, axis=1)


def portions_of(count, total, bound, slope, full):
    portions = [(1 << 20) // math.isqrt(grade ** slope) + 1 for grade in range(1, count + 1)]
    largest = bound if full else min(bound, max(-(-total // count), total * portions[0] // sum(portions)))
    least = 1 if total - largest >= count - 1 else 0
    counts, spare = [largest] + [least] * (count - 1), total - largest - least * (count - 1)
    while spare > 0:
        candidates = [i for i in range(1, count) if counts[i] < largest] or [i for i in range(1, count) if counts[i] < bound]
        whole, remaining = sum([portions[i] for i in candidates]), spare
        for i in candidates:
            extra = min(bound - counts[i], max(1, remaining * portions[i] // whole), spare)
            counts[i] = counts[i] + extra
            spare = spare - extra
    return np.array(counts)


def noise(rng, shape, deviation, most, split=(), kind=jnp.bfloat16):
    values = jax.random.normal(rng, shape, jnp.float32) * deviation
    if len(split) > 0:
        values = block_levels(rng, shape, split, -0.22, 0.18) * values
    return jnp.clip(values, min=-most, max=most).astype(kind)


def setup_inputs(seed: int = 0) -> dict:
    keys = jax.random.split(jax.random.key(seed), 11)
    node_codes = noise(keys[0], (NODES, F), 40.0, 127.0, ((0, 128),))
    node_scales = jnp.clip(jnp.exp(math.log(0.049804688) - 2.3038113 * jax.random.uniform(keys[1], (NODES,), jnp.float32) ** block_levels(keys[1], (NODES,), ((0, 128),), -0.2, 0.2)), 0.0049743652, 0.049804688).astype(jnp.bfloat16)
    target_rows = touch_ends(jax.random.randint(keys[2], (TARGETS,), 0, NODE_DEV), jax.random.fold_in(keys[2], 1), 0, NODE_DEV - 1).astype(jnp.int32)
    owners_keys = jax.random.split(jax.random.fold_in(keys[3], 1), REQS // R_DEV)
    owners_turns = jax.random.permutation(jax.random.fold_in(keys[3], 3), REQS // R_DEV)
    owners = jax.vmap(lambda own, number: routed_block(jax.random.fold_in(keys[3], 2), own, number, R_DEV, N_ROW * N_COL, 1, CAP, 2))(owners_keys, owners_turns).reshape((REQS, 1))
    local_blocks = touch_ends(jax.random.randint(keys[4], (REQS,), 0, NB_DEV), jax.random.fold_in(keys[4], 1), 0, NB_DEV - 1).astype(jnp.int32)
    neighbours = touch_ends(jax.random.randint(keys[5], (TARGETS, K), 0, R_DEV * BR), jax.random.fold_in(keys[5], 1), 0, (R_DEV * BR) - 1).astype(jnp.int32)
    weight_self = noise(keys[6], (F, H), F ** -0.5, 0.21875)
    weight_neigh = noise(keys[7], (F, H), F ** -0.5, 0.21875)
    bias = noise(keys[8], (H,), 0.5, 3.0, (), jnp.float32)
    cotangent = noise(keys[9], (TARGETS, H), (1.0 / (TGT * N_ROW * N_COL) ** 0.5), 0.016479492, ((0, 128),))
    return {"node_codes": node_codes, "node_scales": node_scales, "target_rows": target_rows, "owners": owners, "local_blocks": local_blocks, "neighbours": neighbours, "weight_self": weight_self, "weight_neigh": weight_neigh, "bias": bias, "cotangent": cotangent}


def gelu_value(pre):
    inner = 0.7978845608 * (pre + 0.044715 * pre * pre * pre)
    return 0.5 * pre * (1.0 + jnp.tanh(inner))


def gelu_slope(pre):
    inner = 0.7978845608 * (pre + 0.044715 * pre * pre * pre)
    tangent = jnp.tanh(inner)
    return 0.5 * (1.0 + tangent) + 0.5 * pre * (1.0 - tangent * tangent) * 0.7978845608 * (1.0 + 3.0 * 0.044715 * pre * pre)


def reference(node_codes, node_scales, target_rows, owners, local_blocks, neighbours, weight_self, weight_neigh, bias, cotangent):
    devices = N_ROW * N_COL
    first_owner = owners[:, 0]

    def one_device(carry, device):
        targets = lax.dynamic_slice_in_dim(target_rows, device * TGT, TGT) + device * NODE_DEV
        owned = lax.dynamic_slice_in_dim(first_owner, device * R_DEV, R_DEV)
        located = lax.dynamic_slice_in_dim(local_blocks, device * R_DEV, R_DEV)
        sampled = lax.dynamic_slice_in_dim(neighbours, device * TGT, TGT, 0)
        block_ids = owned * NB_DEV + located
        node_ids = block_ids[sampled // BR] * BR + sampled % BR
        x_self = (node_codes[targets].astype(jnp.float32) * node_scales[targets].astype(jnp.float32)[:, None]).astype(jnp.bfloat16)
        total = jnp.zeros((TGT, F), jnp.float32)
        for step in range(K):
            picked = node_ids[:, step]
            total = total + node_codes[picked].astype(jnp.float32) * node_scales[picked].astype(jnp.float32)[:, None]
        neigh_mean = (total / K).astype(jnp.bfloat16)
        pre = jnp.dot(x_self, weight_self, preferred_element_type=jnp.float32) + jnp.dot(neigh_mean, weight_neigh, preferred_element_type=jnp.float32) + bias
        hidden = gelu_value(pre).astype(jnp.bfloat16)
        upstream = lax.dynamic_slice_in_dim(cotangent, device * TGT, TGT, 0)
        delta = (upstream.astype(jnp.float32) * gelu_slope(pre)).astype(jnp.bfloat16)
        term_self = lax.dot_general(x_self, delta, (((0,), (0,)), ((), ())), preferred_element_type=jnp.float32)
        term_neigh = lax.dot_general(neigh_mean, delta, (((0,), (0,)), ((), ())), preferred_element_type=jnp.float32)
        term_bias = jnp.sum(delta.astype(jnp.float32), axis=0)
        return (carry[0] + term_self, carry[1] + term_neigh, carry[2] + term_bias), hidden

    start = (jnp.zeros((F, H), jnp.float32), jnp.zeros((F, H), jnp.float32), jnp.zeros((H,), jnp.float32))
    sums, outputs = lax.scan(one_device, start, jnp.arange(devices, dtype=jnp.int32))
    return outputs.reshape(TARGETS, H), sums[0], sums[1], sums[2]
```

```python
import jax
import jax.numpy as jnp
from jax import lax
from jax.sharding import Mesh, PartitionSpec as P

BR = 32
K = 10
CAP = 2


def gelu_value(pre):
    inner = 0.7978845608 * (pre + 0.044715 * pre * pre * pre)
    return 0.5 * pre * (1.0 + jnp.tanh(inner))


def gelu_slope(pre):
    inner = 0.7978845608 * (pre + 0.044715 * pre * pre * pre)
    tangent = jnp.tanh(inner)
    return 0.5 * (1.0 + tangent) + 0.5 * pre * (1.0 - tangent * tangent) * 0.7978845608 * (
        1.0 + 3.0 * 0.044715 * pre * pre
    )


def select_rows(indices, count, source):
    columns = jnp.arange(count, dtype=jnp.int32)
    picker = (indices[:, None] == columns[None, :]).astype(jnp.bfloat16)
    return jnp.dot(picker, source, preferred_element_type=jnp.float32).astype(jnp.bfloat16)


ALL = ("z", "core", "x", "y")
CHIPS = ("z", "x", "y")
SWAP = [(0, 1), (1, 0)]


def exchange(array, axes):
    return lax.all_to_all(array, axes, split_axis=0, concat_axis=0, tiled=True)


def pack(term, bias_term):
    rows = term.reshape(8, 96, 8, 128).transpose(0, 2, 1, 3)
    tail = jnp.zeros((8, 8, 16, 128), jnp.float32).at[:, :, 0, :].set(bias_term.reshape(8, 128))
    return jnp.concatenate([rows, tail], axis=2).astype(jnp.bfloat16).reshape(64, 112, 128)


def unpack(chunks):
    rows = chunks.reshape(8, 8, 112, 128)
    grad = rows[:, :, :96, :].transpose(0, 2, 1, 3).reshape(768, 1024).astype(jnp.float32)
    return grad, rows[0, :, 96, :].reshape(1024).astype(jnp.float32)


def sum_over_devices(term_self, term_neigh, term_bias):
    first = lax.axis_index("core") == 0
    packed_self, packed_neigh = pack(term_self, term_bias), pack(term_neigh, term_bias)
    kept = jnp.where(first, packed_self, packed_neigh)
    given = jnp.where(first, packed_neigh, packed_self)
    received = lax.ppermute(given, "core", SWAP)
    chip = (kept.astype(jnp.float32) + received.astype(jnp.float32)).astype(jnp.bfloat16)
    parts = exchange(chip, CHIPS)
    mine = jnp.sum(parts.astype(jnp.float32), axis=0).astype(jnp.bfloat16)
    full = exchange(jnp.broadcast_to(mine[None], (64, 112, 128)), CHIPS)
    theirs = lax.ppermute(full, "core", SWAP)
    grad_self, grad_bias = unpack(jnp.where(first, full, theirs))
    grad_neigh, _ = unpack(jnp.where(first, theirs, full))
    return grad_self, grad_neigh, grad_bias


def local(
    node_codes,
    node_scales,
    target_rows,
    owners,
    local_blocks,
    neighbours,
    weight_self,
    weight_neigh,
    bias,
    cotangent,
):
    devices = lax.axis_size("z") * lax.axis_size("core") * lax.axis_size("x") * lax.axis_size("y")
    width = node_codes.shape[1]
    owned_nodes = node_codes.shape[0]
    block_count = owned_nodes // BR
    first_owner = owners[:, 0]
    requests = first_owner.shape[0]
    order = jnp.arange(requests, dtype=jnp.int32)
    earlier = (first_owner[:, None] == first_owner[None, :]) & (order[None, :] < order[:, None])
    ranking = jnp.sum(earlier.astype(jnp.int32), axis=1)
    slots = first_owner * CAP + ranking
    table = jnp.zeros((devices * CAP,), jnp.int32).at[slots].set(local_blocks)
    asked = exchange(table, ALL)
    values = (
        node_codes.astype(jnp.float32) * node_scales.astype(jnp.float32)[:, None]
    ).astype(jnp.bfloat16)
    blocks = values.reshape(block_count, BR * width)
    send = select_rows(asked, block_count, blocks).reshape(devices * CAP, BR, width)
    got = exchange(send, ALL)
    slot_count = devices * CAP
    pool = select_rows(slots, slot_count, got.reshape(slot_count, BR * width)).reshape(-1, width)
    x_self = select_rows(target_rows, owned_nodes, values)
    pool_rows = pool.shape[0]
    column_ids = jnp.arange(pool_rows, dtype=jnp.int32)
    tally = jnp.zeros((target_rows.shape[0], pool_rows), jnp.float32)
    for step in range(K):
        tally = tally + (neighbours[:, step][:, None] == column_ids[None, :]).astype(jnp.float32)
    tally_half = tally.astype(jnp.bfloat16)
    total = jnp.dot(tally_half, pool, preferred_element_type=jnp.float32)
    neigh_mean = (total / K).astype(jnp.bfloat16)
    pre = (
        jnp.dot(x_self, weight_self, preferred_element_type=jnp.float32)
        + jnp.dot(neigh_mean, weight_neigh, preferred_element_type=jnp.float32)
        + bias
    )
    hidden = gelu_value(pre).astype(jnp.bfloat16)
    delta = (cotangent.astype(jnp.float32) * gelu_slope(pre)).astype(jnp.bfloat16)
    term_self = lax.dot_general(
        x_self, delta, (((0,), (0,)), ((), ())), preferred_element_type=jnp.float32
    )
    term_neigh = lax.dot_general(
        neigh_mean, delta, (((0,), (0,)), ((), ())), preferred_element_type=jnp.float32
    )
    term_bias = jnp.sum(delta.astype(jnp.float32), axis=0)
    grad_self, grad_neigh, grad_bias = sum_over_devices(
        term_self, term_neigh, term_bias
    )
    return (hidden, grad_self, grad_neigh, grad_bias)


def solution(mesh):
    fine = Mesh(mesh.devices.reshape(4, 2, 4, 4), ALL)
    placed = (
        P(ALL, None),
        P(ALL),
        P(ALL),
        P(ALL, None),
        P(ALL),
        P(ALL, None),
        P(),
        P(),
        P(),
        P(ALL, None),
    )
    return jax.shard_map(
        local,
        mesh=fine,
        in_specs=placed,
        out_specs=(P(ALL, None), P(), P(), P()),
        check_vma=False,
    )
```

```python
import jax
import jax.numpy as jnp
from jax import lax
from jax.experimental import pallas as pl
from jax.experimental.pallas import tpu as pltpu
from jax.sharding import Mesh, PartitionSpec as P

F = 768
H = 1024
BR = 32
K = 10
NODE_DEV = 2048
TGT = 1024
NB_DEV = 64
R_DEV = 128
CHIP_COUNT = 64
DEVICES = 128
HALF = F // 2
RQ = R_DEV // 2
ALL = ("z", "core", "x", "y")
CHIPS = ("z", "x", "y")
SWAP = [(0, 1), (1, 0)]
HB = 256
RB = 96
RBP = 112


def exchange(array, axes):
    return lax.all_to_all(array, axes, split_axis=0, concat_axis=0, tiled=True)


def select_rows(indices, count, source):
    columns = jnp.arange(count, dtype=jnp.int32)
    picker = (indices[:, None] == columns[None, :]).astype(jnp.bfloat16)
    return jnp.dot(picker, source, preferred_element_type=jnp.float32).astype(jnp.bfloat16)


def stripe_kernel(codes_ref, scales_ref, values_ref, stripes_ref, wide):
    wide[...] = codes_ref[...].astype(jnp.float32) * scales_ref[...]
    values_ref[...] = wide[...].astype(jnp.bfloat16)
    for row in range(BR):
        stripes_ref[row, 0] = wide[pl.ds(row, NB_DEV, stride=BR), :].astype(jnp.bfloat16)


def make_stripes(codes, scales):
    return pl.pallas_call(
        stripe_kernel,
        grid=(6,),
        in_specs=[
            pl.BlockSpec((NODE_DEV, 128), lambda k: (0, k)),
            pl.BlockSpec((NODE_DEV, 1), lambda k: (0, 0)),
        ],
        out_specs=[
            pl.BlockSpec((NODE_DEV, 128), lambda k: (0, k)),
            pl.BlockSpec((BR, 1, NB_DEV, 128), lambda k: (0, k // 3, 0, k % 3)),
        ],
        out_shape=[
            jax.ShapeDtypeStruct((NODE_DEV, F), jnp.bfloat16),
            jax.ShapeDtypeStruct((BR, 2, NB_DEV, HALF), jnp.bfloat16),
        ],
        scratch_shapes=[pltpu.VMEM((NODE_DEV, 128), jnp.float32)],
        compiler_params=pltpu.CompilerParams(vmem_limit_bytes=32 << 20),
        name="make_stripes",
    )(codes, scales)


GROUP = 8
TABLE = CHIP_COUNT * NB_DEV


def gather_kernel(wanted_ref, own_ref, sister_ref, out_ref, t0, t1, t2, g0, g1, g2):
    tables, picked = (t0, t1, t2), (g0, g1, g2)

    @pl.when(pl.program_id(0) == 0)
    def _():
        for k in range(3):
            for part, source in enumerate((own_ref, sister_ref)):
                tables[k][pl.ds(part * TABLE, TABLE), :] = source[
                    :, k * 128 : (k + 1) * 128
                ].astype(jnp.float32)

    first = pl.program_id(0) * GROUP

    def one(step, carry):
        for j in range(RQ):
            at = wanted_ref[first + step, j]
            for k in range(3):
                picked[k][pl.ds(j, 1), :] = tables[k][pl.ds(at, 1), :]
        for k in range(3):
            out_ref[step, :, k * 128 : (k + 1) * 128] = picked[k][...].astype(jnp.bfloat16)
        return carry

    lax.fori_loop(0, GROUP, one, 0)


def gather(wanted, own, sister):
    return pl.pallas_call(
        gather_kernel,
        grid_spec=pltpu.PrefetchScalarGridSpec(
            num_scalar_prefetch=1,
            grid=(DEVICES // GROUP,),
            in_specs=[
                pl.BlockSpec((TABLE, HALF), lambda i, w: (0, 0), pipeline_mode=pl.Buffered(1)),
                pl.BlockSpec((TABLE, HALF), lambda i, w: (0, 0), pipeline_mode=pl.Buffered(1)),
            ],
            out_specs=pl.BlockSpec((GROUP, RQ, HALF), lambda i, w: (i, 0, 0)),
            scratch_shapes=[pltpu.VMEM((2 * TABLE, 128), jnp.float32)] * 3
            + [pltpu.VMEM((RQ, 128), jnp.float32)] * 3,
        ),
        out_shape=jax.ShapeDtypeStruct((DEVICES, RQ, HALF), jnp.bfloat16),
        compiler_params=pltpu.CompilerParams(vmem_limit_bytes=40 << 20),
        name="gather_rows",
    )(wanted, own, sister)


MEAN_STEPS = 8
COLS = 2 * BR * R_DEV // 2 // MEAN_STEPS


def layer_kernel(
    core_ref, got_ref, tally_ref, pre_ref, x_t_ref, weight_ref, cot_ref,
    hidden_ref, kept_ref, given_ref, acc, mean, mean_t,
):
    step = pl.program_id(0)

    @pl.when(step < MEAN_STEPS)
    def _():
        counts = tally_ref[...]
        for half in range(2):
            rows = jnp.concatenate(
                [got_ref[2 * e + half] for e in range(8)], axis=0
            )
            part = jnp.dot(counts, rows, preferred_element_type=jnp.float32)

            @pl.when(step == 0)
            def _():
                acc[half] = part

            @pl.when(step > 0)
            def _():
                acc[half] += part

    @pl.when(step == MEAN_STEPS - 1)
    def _():
        for half in range(2):
            value = (acc[half] / K).astype(jnp.bfloat16)
            mean[:, half * HALF : (half + 1) * HALF] = value
            mean_t[half * HALF : (half + 1) * HALF, :] = value.T

    @pl.when(step >= MEAN_STEPS)
    def _():
        pre = pre_ref[...] + jnp.dot(
            mean[...], weight_ref[...], preferred_element_type=jnp.float32
        )
        square = pre * pre
        tangent = jnp.tanh(0.7978845608 * (pre + 0.044715 * pre * square))
        rest = 1.0 + tangent
        hidden_ref[...] = (0.5 * pre * rest).astype(jnp.bfloat16)
        slope = 0.5 * rest + 0.5 * pre * (1.0 - tangent * tangent) * 0.7978845608 * (
            1.0 + 3.0 * 0.044715 * square
        )
        wide = cot_ref[...].astype(jnp.float32) * slope
        delta = wide.astype(jnp.bfloat16)
        bias_term = jnp.sum(delta.astype(jnp.float32), axis=0, keepdims=True)
        first = core_ref[0] == 0
        grad_self = jnp.dot(x_t_ref[...], delta, preferred_element_type=jnp.float32)
        grad_neigh = jnp.dot(mean_t[...], delta, preferred_element_type=jnp.float32)
        tail = jnp.broadcast_to(bias_term, (RBP - RB, HB)).astype(jnp.bfloat16)
        for ref, value in (
            (kept_ref, jnp.where(first, grad_self, grad_neigh)),
            (given_ref, jnp.where(first, grad_neigh, grad_self)),
        ):
            value = value.astype(jnp.bfloat16)
            for c in range(HB // 128):
                lanes = slice(c * 128, (c + 1) * 128)
                for r in range(8):
                    ref[r, c, :RB, :] = value[r * RB : (r + 1) * RB, lanes]
                    ref[r, c, RB:, :] = tail[:, lanes]


def layer(core, got, tally, pre_self, x_t, weight_neigh, cotangent):
    last = MEAN_STEPS - 1
    early = lambda i, w: jnp.minimum(i, last)
    late = lambda i, w: jnp.maximum(i - MEAN_STEPS, 0)
    term = pl.BlockSpec((8, HB // 128, RBP, 128), lambda i, w: (0, late(i, w), 0, 0))
    return pl.pallas_call(
        layer_kernel,
        grid_spec=pltpu.PrefetchScalarGridSpec(
            num_scalar_prefetch=1,
            grid=(MEAN_STEPS + H // HB,),
            in_specs=[
                pl.BlockSpec((16, RQ, HALF), lambda i, w: (early(i, w), 0, 0)),
                pl.BlockSpec((TGT, COLS), lambda i, w: (0, early(i, w))),
                pl.BlockSpec((TGT, HB), lambda i, w: (0, late(i, w))),
                pl.BlockSpec((F, TGT), lambda i, w: (0, 0)),
                pl.BlockSpec((F, HB), lambda i, w: (0, late(i, w))),
                pl.BlockSpec((TGT, HB), lambda i, w: (0, late(i, w))),
            ],
            out_specs=[pl.BlockSpec((TGT, HB), lambda i, w: (0, late(i, w))), term, term],
            scratch_shapes=[
                pltpu.VMEM((2, TGT, HALF), jnp.float32),
                pltpu.VMEM((TGT, F), jnp.bfloat16),
                pltpu.VMEM((F, TGT), jnp.bfloat16),
            ],
        ),
        out_shape=[
            jax.ShapeDtypeStruct((TGT, H), jnp.bfloat16),
            jax.ShapeDtypeStruct((8, 8, RBP, 128), jnp.bfloat16),
            jax.ShapeDtypeStruct((8, 8, RBP, 128), jnp.bfloat16),
        ],
        compiler_params=pltpu.CompilerParams(vmem_limit_bytes=56 << 20),
        name="layer",
    )(core, got, tally, pre_self, x_t, weight_neigh, cotangent)


def unpack(chunks):
    rows = chunks.reshape(8, 8, RBP, 128)
    grad = rows[:, :, :RB, :].transpose(0, 2, 1, 3).reshape(F, H).astype(jnp.float32)
    return grad, rows[0, :, RB, :].reshape(H).astype(jnp.float32)


def sum_over_devices(kept, given, first):
    kept = kept.reshape(CHIP_COUNT, RBP, 128)
    received = lax.ppermute(given.reshape(CHIP_COUNT, RBP, 128), "core", SWAP)
    chip = (kept.astype(jnp.float32) + received.astype(jnp.float32)).astype(jnp.bfloat16)
    parts = exchange(chip, CHIPS)
    mine = jnp.sum(parts.astype(jnp.float32), axis=0).astype(jnp.bfloat16)
    full = exchange(jnp.broadcast_to(mine[None], (CHIP_COUNT, RBP, 128)), CHIPS)
    theirs = lax.ppermute(full, "core", SWAP)
    grad_self, grad_bias = unpack(jnp.where(first, full, theirs))
    grad_neigh, _ = unpack(jnp.where(first, theirs, full))
    return grad_self, grad_neigh, grad_bias


def local(
    node_codes, node_scales, target_rows, owners, local_blocks, neighbours,
    weight_self, weight_neigh, bias, cotangent,
):
    core = lax.axis_index("core")
    owner = owners[:, 0]
    owner_core = (owner // 16) % 2
    owner_chip = (owner // 32) * 16 + owner % 16
    serving = (jnp.arange(R_DEV, dtype=jnp.int32) // RQ) % 2
    place = (owner_core != serving).astype(jnp.int32) * TABLE + owner_chip * NB_DEV + local_blocks
    asked = jnp.broadcast_to(place.reshape(1, 2, 1, RQ), (4, 2, 16, RQ)).reshape(DEVICES, RQ)
    wanted = exchange(asked, ALL)

    values, stripes = make_stripes(node_codes, node_scales.astype(jnp.float32)[:, None])
    own = exchange(stripes.reshape(CHIP_COUNT, NB_DEV, HALF), CHIPS)
    own = own.reshape(TABLE, HALF)
    sister = lax.ppermute(own, "core", SWAP)
    got = exchange(gather(wanted, own, sister), ALL)

    x_self = select_rows(target_rows, NODE_DEV, values)
    pre_self = jnp.dot(x_self, weight_self, preferred_element_type=jnp.float32) + bias
    block, row = neighbours // BR, neighbours % BR
    column = (row // 8) * 1024 + (block // RQ) * 512 + (row % 8) * RQ + block % RQ
    ids = jnp.arange(R_DEV * BR, dtype=jnp.int32)
    tally = jnp.zeros((TGT, R_DEV * BR), jnp.float32)
    for step in range(K):
        tally = tally + (column[:, step][:, None] == ids[None, :]).astype(jnp.float32)

    hidden, kept, given = layer(
        core.reshape(1).astype(jnp.int32), got, tally.astype(jnp.bfloat16), pre_self, x_self.T,
        weight_neigh, cotangent,
    )
    return (hidden,) + sum_over_devices(kept, given, core == 0)


def solution(mesh):
    fine = Mesh(mesh.devices.reshape(4, 2, 4, 4), ALL)
    placed = (
        P(ALL, None),
        P(ALL),
        P(ALL),
        P(ALL, None),
        P(ALL),
        P(ALL, None),
        P(),
        P(),
        P(),
        P(ALL, None),
    )
    return jax.shard_map(
        local,
        mesh=fine,
        in_specs=placed,
        out_specs=(P(ALL, None), P(), P(), P()),
        check_vma=False,
    )
```

```python
import jax
import jax.numpy as jnp
from jax import lax
from jax.experimental import pallas as pl
from jax.experimental.pallas import tpu as pltpu
from jax.sharding import Mesh, PartitionSpec as P

F = 768
H = 1024
BR = 32
K = 10
NODE_DEV = 2048
TGT = 1024
NB_DEV = 64
R_DEV = 128
CHIP_COUNT = 64
DEVICES = 128
HALF = F // 2
RQ = R_DEV // 2
ALL = ("z", "core", "x", "y")
CHIPS = ("z", "x", "y")
SWAP = [(0, 1), (1, 0)]
HB = 256
RB = 96
RBP = 112


def exchange(array, axes):
    return lax.all_to_all(array, axes, split_axis=0, concat_axis=0, tiled=True)


def select_rows(indices, count, source):
    columns = jnp.arange(count, dtype=jnp.int32)
    picker = (indices[:, None] == columns[None, :]).astype(jnp.bfloat16)
    return jnp.dot(picker, source, preferred_element_type=jnp.float32).astype(jnp.bfloat16)


def stripe_kernel(codes_ref, scales_ref, values_ref, stripes_ref, wide):
    wide[...] = codes_ref[...].astype(jnp.float32) * scales_ref[...]
    values_ref[...] = wide[...].astype(jnp.bfloat16)
    for row in range(BR):
        stripes_ref[row, 0] = wide[pl.ds(row, NB_DEV, stride=BR), :].astype(jnp.bfloat16)


def make_stripes(codes, scales):
    return pl.pallas_call(
        stripe_kernel,
        grid=(6,),
        in_specs=[
            pl.BlockSpec((NODE_DEV, 128), lambda k: (0, k)),
            pl.BlockSpec((NODE_DEV, 1), lambda k: (0, 0)),
        ],
        out_specs=[
            pl.BlockSpec((NODE_DEV, 128), lambda k: (0, k)),
            pl.BlockSpec((BR, 1, NB_DEV, 128), lambda k: (0, k // 3, 0, k % 3)),
        ],
        out_shape=[
            jax.ShapeDtypeStruct((NODE_DEV, F), jnp.bfloat16),
            jax.ShapeDtypeStruct((BR, 2, NB_DEV, HALF), jnp.bfloat16),
        ],
        scratch_shapes=[pltpu.VMEM((NODE_DEV, 128), jnp.float32)],
        compiler_params=pltpu.CompilerParams(vmem_limit_bytes=60 << 20),
        name="make_stripes",
    )(codes, scales)


GROUP = 16
TABLE = CHIP_COUNT * NB_DEV
SLOT = 4


def gather_kernel(wanted_ref, own_ref, sister_ref, out_ref, table, picked):
    @pl.when(pl.program_id(0) == 0)
    def _():
        for part, source in enumerate((own_ref, sister_ref)):
            for k in range(3):
                table[pl.ds(part * TABLE * SLOT + k, TABLE, stride=SLOT), :] = source[
                    :, k * 128 : (k + 1) * 128
                ].astype(jnp.float32)

    first = pl.program_id(0) * GROUP

    def pair(step, carry):
        for u in range(2):
            base = u * RQ * SLOT
            for j in range(RQ):
                at = pl.multiple_of(wanted_ref[first + 2 * step + u, j], SLOT)
                picked[pl.ds(base + j * SLOT, SLOT), :] = table[pl.ds(at, SLOT), :]
            for k in range(3):
                out_ref[2 * step + u, :, k * 128 : (k + 1) * 128] = picked[
                    pl.ds(base + k, RQ, stride=SLOT), :
                ].astype(jnp.bfloat16)
        return carry

    lax.fori_loop(0, GROUP // 2, pair, 0)


def gather(wanted, own, sister):
    return pl.pallas_call(
        gather_kernel,
        grid_spec=pltpu.PrefetchScalarGridSpec(
            num_scalar_prefetch=1,
            grid=(DEVICES // GROUP,),
            in_specs=[
                pl.BlockSpec((TABLE, HALF), lambda i, w: (0, 0), pipeline_mode=pl.Buffered(1)),
                pl.BlockSpec((TABLE, HALF), lambda i, w: (0, 0), pipeline_mode=pl.Buffered(1)),
            ],
            out_specs=pl.BlockSpec((GROUP, RQ, HALF), lambda i, w: (i, 0, 0)),
            scratch_shapes=[
                pltpu.VMEM((2 * TABLE * SLOT, 128), jnp.float32),
                pltpu.VMEM((2 * RQ * SLOT, 128), jnp.float32),
            ],
        ),
        out_shape=jax.ShapeDtypeStruct((DEVICES, RQ, HALF), jnp.bfloat16),
        compiler_params=pltpu.CompilerParams(vmem_limit_bytes=60 << 20),
        name="gather_rows",
    )(wanted, own, sister)


MEAN_STEPS = 8
COLS = 2 * BR * R_DEV // 2 // MEAN_STEPS


def layer_kernel(
    core_ref, got_ref, tally_ref, pre_ref, x_t_ref, weight_ref, cot_ref,
    hidden_ref, kept_ref, given_ref, acc, mean, mean_t,
):
    step = pl.program_id(0)

    @pl.when(step < MEAN_STEPS)
    def _():
        rows = jnp.concatenate(
            [
                jnp.concatenate([got_ref[2 * e + half] for e in range(8)], axis=0)
                for half in range(2)
            ],
            axis=1,
        )
        part = jnp.dot(tally_ref[...], rows, preferred_element_type=jnp.float32)

        @pl.when(step == 0)
        def _():
            acc[...] = part

        @pl.when(step > 0)
        def _():
            acc[...] += part

    @pl.when(step == MEAN_STEPS - 1)
    def _():
        value = (acc[...] / K).astype(jnp.bfloat16)
        mean[...] = value
        mean_t[...] = value.T

    @pl.when(step >= MEAN_STEPS)
    def _():
        pre = pre_ref[...] + jnp.dot(
            mean[...], weight_ref[...], preferred_element_type=jnp.float32
        )
        square = pre * pre
        tangent = jnp.tanh(0.7978845608 * (pre + 0.044715 * pre * square))
        rest = 1.0 + tangent
        hidden_ref[...] = (0.5 * pre * rest).astype(jnp.bfloat16)
        slope = 0.5 * rest + 0.5 * pre * (1.0 - tangent * tangent) * 0.7978845608 * (
            1.0 + 3.0 * 0.044715 * square
        )
        wide = cot_ref[...].astype(jnp.float32) * slope
        delta = wide.astype(jnp.bfloat16)
        bias_term = jnp.sum(delta.astype(jnp.float32), axis=0, keepdims=True)
        first = core_ref[0] == 0
        grad_self = jnp.dot(x_t_ref[...], delta, preferred_element_type=jnp.float32)
        grad_neigh = jnp.dot(mean_t[...], delta, preferred_element_type=jnp.float32)
        tail = jnp.broadcast_to(bias_term, (RBP - RB, HB)).astype(jnp.bfloat16)
        for ref, value in (
            (kept_ref, jnp.where(first, grad_self, grad_neigh)),
            (given_ref, jnp.where(first, grad_neigh, grad_self)),
        ):
            value = value.astype(jnp.bfloat16)
            for c in range(HB // 128):
                lanes = slice(c * 128, (c + 1) * 128)
                for r in range(8):
                    ref[r, c, :RB, :] = value[r * RB : (r + 1) * RB, lanes]
                    ref[r, c, RB:, :] = tail[:, lanes]


def layer(core, got, tally, pre_self, x_t, weight_neigh, cotangent):
    last = MEAN_STEPS - 1
    early = lambda i, w: jnp.minimum(i, last)
    late = lambda i, w: jnp.maximum(i - MEAN_STEPS, 0)
    term = pl.BlockSpec((8, HB // 128, RBP, 128), lambda i, w: (0, late(i, w), 0, 0))
    return pl.pallas_call(
        layer_kernel,
        grid_spec=pltpu.PrefetchScalarGridSpec(
            num_scalar_prefetch=1,
            grid=(MEAN_STEPS + H // HB,),
            in_specs=[
                pl.BlockSpec((16, RQ, HALF), lambda i, w: (early(i, w), 0, 0)),
                pl.BlockSpec((TGT, COLS), lambda i, w: (0, early(i, w))),
                pl.BlockSpec((TGT, HB), lambda i, w: (0, late(i, w))),
                pl.BlockSpec((F, TGT), lambda i, w: (0, 0)),
                pl.BlockSpec((F, HB), lambda i, w: (0, late(i, w))),
                pl.BlockSpec((TGT, HB), lambda i, w: (0, late(i, w))),
            ],
            out_specs=[pl.BlockSpec((TGT, HB), lambda i, w: (0, late(i, w))), term, term],
            scratch_shapes=[
                pltpu.VMEM((TGT, F), jnp.float32),
                pltpu.VMEM((TGT, F), jnp.bfloat16),
                pltpu.VMEM((F, TGT), jnp.bfloat16),
            ],
        ),
        out_shape=[
            jax.ShapeDtypeStruct((TGT, H), jnp.bfloat16),
            jax.ShapeDtypeStruct((8, 8, RBP, 128), jnp.bfloat16),
            jax.ShapeDtypeStruct((8, 8, RBP, 128), jnp.bfloat16),
        ],
        compiler_params=pltpu.CompilerParams(vmem_limit_bytes=56 << 20),
        name="layer",
    )(core, got, tally, pre_self, x_t, weight_neigh, cotangent)


def unpack_kernel(core_ref, full_ref, theirs_ref, self_ref, neigh_ref, bias_ref):
    first = core_ref[0] == 0
    for c in range(8):
        lanes = slice(c * 128, (c + 1) * 128)
        a = full_ref[0, c].astype(jnp.float32)
        b = theirs_ref[0, c].astype(jnp.float32)
        self_ref[:, lanes] = jnp.where(first, a[:RB], b[:RB])
        neigh_ref[:, lanes] = jnp.where(first, b[:RB], a[:RB])
        bias_ref[:, lanes] = a[RB : RB + 1]


def unpack(core, full, theirs):
    chunks = pl.BlockSpec((1, 8, RBP, 128), lambda i, w: (i, 0, 0, 0))
    return pl.pallas_call(
        unpack_kernel,
        grid_spec=pltpu.PrefetchScalarGridSpec(
            num_scalar_prefetch=1,
            grid=(8,),
            in_specs=[chunks, chunks],
            out_specs=[
                pl.BlockSpec((RB, H), lambda i, w: (i, 0)),
                pl.BlockSpec((RB, H), lambda i, w: (i, 0)),
                pl.BlockSpec((1, H), lambda i, w: (0, 0)),
            ],
        ),
        out_shape=[
            jax.ShapeDtypeStruct((F, H), jnp.float32),
            jax.ShapeDtypeStruct((F, H), jnp.float32),
            jax.ShapeDtypeStruct((1, H), jnp.float32),
        ],
        compiler_params=pltpu.CompilerParams(vmem_limit_bytes=60 << 20),
        name="unpack",
    )(core, full.reshape(8, 8, RBP, 128), theirs.reshape(8, 8, RBP, 128))


def sum_over_devices(kept, given, core):
    kept = kept.reshape(CHIP_COUNT, RBP, 128)
    received = lax.ppermute(given.reshape(CHIP_COUNT, RBP, 128), "core", SWAP)
    chip = (kept.astype(jnp.float32) + received.astype(jnp.float32)).astype(jnp.bfloat16)
    parts = exchange(chip, CHIPS)
    mine = jnp.sum(parts.astype(jnp.float32), axis=0).astype(jnp.bfloat16)
    full = exchange(jnp.broadcast_to(mine[None], (CHIP_COUNT, RBP, 128)), CHIPS)
    theirs = lax.ppermute(full, "core", SWAP)
    grad_self, grad_neigh, grad_bias = unpack(core, full, theirs)
    return grad_self, grad_neigh, grad_bias.reshape(H)


def local(
    node_codes, node_scales, target_rows, owners, local_blocks, neighbours,
    weight_self, weight_neigh, bias, cotangent,
):
    core = lax.axis_index("core")
    owner = owners[:, 0]
    owner_core = (owner // 16) % 2
    owner_chip = (owner // 32) * 16 + owner % 16
    serving = (jnp.arange(R_DEV, dtype=jnp.int32) // RQ) % 2
    place = (owner_core != serving).astype(jnp.int32) * TABLE + owner_chip * NB_DEV + local_blocks
    place = place * SLOT
    asked = jnp.broadcast_to(place.reshape(1, 2, 1, RQ), (4, 2, 16, RQ)).reshape(DEVICES, RQ)
    wanted = exchange(asked, ALL)

    values, stripes = make_stripes(node_codes, node_scales.astype(jnp.float32)[:, None])
    own = exchange(stripes.reshape(CHIP_COUNT, NB_DEV, HALF), CHIPS)
    own = own.reshape(TABLE, HALF)
    sister = lax.ppermute(own, "core", SWAP)
    got = exchange(gather(wanted, own, sister), ALL)

    x_self = select_rows(target_rows, NODE_DEV, values)
    pre_self = jnp.dot(x_self, weight_self, preferred_element_type=jnp.float32) + bias
    block, row = neighbours // BR, neighbours % BR
    column = (row // 8) * 1024 + (block // RQ) * 512 + (row % 8) * RQ + block % RQ
    ids = jnp.arange(R_DEV * BR, dtype=jnp.int32)
    tally = jnp.zeros((TGT, R_DEV * BR), jnp.float32)
    for step in range(K):
        tally = tally + (column[:, step][:, None] == ids[None, :]).astype(jnp.float32)

    which = core.reshape(1).astype(jnp.int32)
    hidden, kept, given = layer(
        which, got, tally.astype(jnp.bfloat16), pre_self, x_self.T, weight_neigh, cotangent
    )
    return (hidden,) + sum_over_devices(kept, given, which)


def solution(mesh):
    fine = Mesh(mesh.devices.reshape(4, 2, 4, 4), ALL)
    placed = (
        P(ALL, None),
        P(ALL),
        P(ALL),
        P(ALL, None),
        P(ALL),
        P(ALL, None),
        P(),
        P(),
        P(),
        P(ALL, None),
    )
    return jax.shard_map(
        local,
        mesh=fine,
        in_specs=placed,
        out_specs=(P(ALL, None), P(), P(), P()),
        check_vma=False,
    )
```

```python
import jax
import jax.numpy as jnp
from jax import lax
from jax.experimental import pallas as pl
from jax.experimental.pallas import tpu as pltpu
from jax.sharding import Mesh, PartitionSpec as P

F = 768
H = 1024
BR = 32
K = 10
NODE_DEV = 2048
TGT = 1024
NB_DEV = 64
R_DEV = 128
CHIP_COUNT = 64
DEVICES = 128
HALF = F // 2
RQ = R_DEV // 2
ALL = ("z", "core", "x", "y")
CHIPS = ("z", "x", "y")
SWAP = [(0, 1), (1, 0)]
HB = 256
RB = 96
RBP = 112


def exchange(array, axes):
    return lax.all_to_all(array, axes, split_axis=0, concat_axis=0, tiled=True)


def select_rows(indices, count, source):
    columns = jnp.arange(count, dtype=jnp.int32)
    picker = (indices[:, None] == columns[None, :]).astype(jnp.bfloat16)
    return jnp.dot(picker, source, preferred_element_type=jnp.float32).astype(jnp.bfloat16)


def stripe_copy(codes_ref, codes, sem, k):
    lanes = pl.ds(pl.multiple_of(k * 128, 128), 128)
    return pltpu.make_async_copy(codes_ref.at[:, lanes], codes.at[k], sem.at[k])


def stripe_kernel(codes_ref, scales_ref, stripes_ref, codes, scales, wide, sem):
    k = pl.program_id(0)

    @pl.when(k == 0)
    def _():
        for n in range(6):
            stripe_copy(codes_ref, codes, sem, n).start()
        columns = scales_ref[...].T
        for c in range(NODE_DEV // 128):
            scales[c * 128 : (c + 1) * 128, :] = jnp.broadcast_to(columns[:, c : c + 1], (128, 128))

    stripe_copy(codes_ref, codes, sem, k).wait()
    wide[...] = codes[k].astype(jnp.float32) * scales[...]
    for row in range(BR):
        stripes_ref[row, 0] = wide[pl.ds(row, NB_DEV, stride=BR), :].astype(jnp.bfloat16)


def make_stripes(codes, scales):
    return pl.pallas_call(
        stripe_kernel,
        grid=(6,),
        in_specs=[
            pl.BlockSpec(memory_space=pltpu.HBM),
            pl.BlockSpec((NODE_DEV // 128, 128), lambda k: (0, 0)),
        ],
        out_specs=pl.BlockSpec((BR, 1, NB_DEV, 128), lambda k: (0, k // 3, 0, k % 3)),
        out_shape=jax.ShapeDtypeStruct((BR, 2, NB_DEV, HALF), jnp.bfloat16),
        scratch_shapes=[
            pltpu.VMEM((6, NODE_DEV, 128), jnp.bfloat16),
            pltpu.VMEM((NODE_DEV, 128), jnp.float32),
            pltpu.VMEM((NODE_DEV, 128), jnp.float32),
            pltpu.SemaphoreType.DMA((6,)),
        ],
        compiler_params=pltpu.CompilerParams(vmem_limit_bytes=12 << 20),
        name="make_stripes",
    )(codes, scales.reshape(NODE_DEV // 128, 128))


GROUP = 16
TABLE = CHIP_COUNT * NB_DEV
SLOT = 4


def gather_kernel(wanted_ref, own_ref, sister_ref, out_ref, table, picked):
    @pl.when(pl.program_id(0) == 0)
    def _():
        for part, source in enumerate((own_ref, sister_ref)):
            for k in range(3):
                table[pl.ds(part * TABLE * SLOT + k, TABLE, stride=SLOT), :] = source[
                    :, k * 128 : (k + 1) * 128
                ].astype(jnp.float32)

    first = pl.program_id(0) * GROUP

    def pair(step, carry):
        for u in range(2):
            base = u * RQ * SLOT
            for j in range(RQ):
                at = pl.multiple_of(wanted_ref[first + 2 * step + u, j], SLOT)
                picked[pl.ds(base + j * SLOT, SLOT), :] = table[pl.ds(at, SLOT), :]
            for k in range(3):
                out_ref[2 * step + u, :, k * 128 : (k + 1) * 128] = picked[
                    pl.ds(base + k, RQ, stride=SLOT), :
                ].astype(jnp.bfloat16)
        return carry

    lax.fori_loop(0, GROUP // 2, pair, 0)


def gather(wanted, own, sister):
    return pl.pallas_call(
        gather_kernel,
        grid_spec=pltpu.PrefetchScalarGridSpec(
            num_scalar_prefetch=1,
            grid=(DEVICES // GROUP,),
            in_specs=[
                pl.BlockSpec((TABLE, HALF), lambda i, w: (0, 0), pipeline_mode=pl.Buffered(1)),
                pl.BlockSpec((TABLE, HALF), lambda i, w: (0, 0), pipeline_mode=pl.Buffered(1)),
            ],
            out_specs=pl.BlockSpec((GROUP, RQ, HALF), lambda i, w: (i, 0, 0)),
            scratch_shapes=[
                pltpu.VMEM((2 * TABLE * SLOT, 128), jnp.float32),
                pltpu.VMEM((2 * RQ * SLOT, 128), jnp.float32),
            ],
        ),
        out_shape=pltpu.HBM((DEVICES, RQ, HALF), jnp.bfloat16),
        compiler_params=pltpu.CompilerParams(vmem_limit_bytes=27 << 20),
        name="gather_rows",
    )(wanted, own, sister)


MEAN_STEPS = 4
COLS = 2 * BR * R_DEV // 2 // MEAN_STEPS


def layer_kernel(
    core_ref, got_ref, tally_ref, pre_ref, x_t_ref, weight_ref, cot_ref,
    hidden_ref, kept_ref, given_ref, acc, mean, mean_t,
):
    step = pl.program_id(0)

    @pl.when(step < MEAN_STEPS)
    def _():
        rows = jnp.concatenate(
            [
                jnp.concatenate([got_ref[2 * e + half] for e in range(COLS // RQ)], axis=0)
                for half in range(2)
            ],
            axis=1,
        )
        part = jnp.dot(tally_ref[...], rows, preferred_element_type=jnp.float32)

        @pl.when(step == 0)
        def _():
            acc[...] = part

        @pl.when(step > 0)
        def _():
            acc[...] += part

    @pl.when(step == MEAN_STEPS - 1)
    def _():
        value = (acc[...] / K).astype(jnp.bfloat16)
        mean[...] = value
        mean_t[...] = value.T

    @pl.when(step >= MEAN_STEPS)
    def _():
        pre = pre_ref[...] + jnp.dot(
            mean[...], weight_ref[...], preferred_element_type=jnp.float32
        )
        square = pre * pre
        tangent = jnp.tanh(0.7978845608 * (pre + 0.044715 * pre * square))
        rest = 1.0 + tangent
        hidden_ref[...] = (0.5 * pre * rest).astype(jnp.bfloat16)
        slope = 0.5 * rest + 0.5 * pre * (1.0 - tangent * tangent) * 0.7978845608 * (
            1.0 + 3.0 * 0.044715 * square
        )
        wide = cot_ref[...].astype(jnp.float32) * slope
        delta = wide.astype(jnp.bfloat16)
        bias_term = jnp.sum(delta.astype(jnp.float32), axis=0, keepdims=True)
        first = core_ref[0] == 0
        grad_self = jnp.dot(x_t_ref[...], delta, preferred_element_type=jnp.float32)
        grad_neigh = jnp.dot(mean_t[...], delta, preferred_element_type=jnp.float32)
        tail = jnp.broadcast_to(bias_term, (RBP - RB, HB)).astype(jnp.bfloat16)
        for ref, value in (
            (kept_ref, jnp.where(first, grad_self, grad_neigh)),
            (given_ref, jnp.where(first, grad_neigh, grad_self)),
        ):
            value = value.astype(jnp.bfloat16)
            for c in range(HB // 128):
                lanes = slice(c * 128, (c + 1) * 128)
                for r in range(8):
                    ref[r, c, :RB, :] = value[r * RB : (r + 1) * RB, lanes]
                    ref[r, c, RB:, :] = tail[:, lanes]


def layer(core, got, tally, pre_self, x_t, weight_neigh, cotangent):
    last = MEAN_STEPS - 1
    early = lambda i, w: jnp.minimum(i, last)
    late = lambda i, w: jnp.maximum(i - MEAN_STEPS, 0)
    term = pl.BlockSpec((8, HB // 128, RBP, 128), lambda i, w: (0, late(i, w), 0, 0))
    return pl.pallas_call(
        layer_kernel,
        grid_spec=pltpu.PrefetchScalarGridSpec(
            num_scalar_prefetch=1,
            grid=(MEAN_STEPS + H // HB,),
            in_specs=[
                pl.BlockSpec((DEVICES // MEAN_STEPS, RQ, HALF), lambda i, w: (early(i, w), 0, 0)),
                pl.BlockSpec((TGT, COLS), lambda i, w: (0, early(i, w))),
                pl.BlockSpec((TGT, HB), lambda i, w: (0, late(i, w))),
                pl.BlockSpec((F, TGT), lambda i, w: (0, 0)),
                pl.BlockSpec((F, HB), lambda i, w: (0, late(i, w))),
                pl.BlockSpec((TGT, HB), lambda i, w: (0, late(i, w))),
            ],
            out_specs=[pl.BlockSpec((TGT, HB), lambda i, w: (0, late(i, w))), term, term],
            scratch_shapes=[
                pltpu.VMEM((TGT, F), jnp.float32),
                pltpu.VMEM((TGT, F), jnp.bfloat16),
                pltpu.VMEM((F, TGT), jnp.bfloat16),
            ],
        ),
        out_shape=[
            jax.ShapeDtypeStruct((TGT, H), jnp.bfloat16),
            jax.ShapeDtypeStruct((8, 8, RBP, 128), jnp.bfloat16),
            jax.ShapeDtypeStruct((8, 8, RBP, 128), jnp.bfloat16),
        ],
        compiler_params=pltpu.CompilerParams(vmem_limit_bytes=28 << 20),
        name="layer",
    )(core, got, tally, pre_self, x_t, weight_neigh, cotangent)


def unpack_kernel(core_ref, full_ref, theirs_ref, self_ref, neigh_ref, bias_ref):
    first = core_ref[0] == 0
    for r in range(2):
        rows = slice(r * RB, (r + 1) * RB)
        for c in range(8):
            lanes = slice(c * 128, (c + 1) * 128)
            a = full_ref[r, c].astype(jnp.float32)
            b = theirs_ref[r, c].astype(jnp.float32)
            self_ref[rows, lanes] = jnp.where(first, a[:RB], b[:RB])
            neigh_ref[rows, lanes] = jnp.where(first, b[:RB], a[:RB])
            bias_ref[:, lanes] = a[RB : RB + 1]


def unpack(core, full, theirs):
    chunks = pl.BlockSpec((2, 8, RBP, 128), lambda i, w: (i, 0, 0, 0))
    return pl.pallas_call(
        unpack_kernel,
        grid_spec=pltpu.PrefetchScalarGridSpec(
            num_scalar_prefetch=1,
            grid=(4,),
            in_specs=[chunks, chunks],
            out_specs=[
                pl.BlockSpec((2 * RB, H), lambda i, w: (i, 0)),
                pl.BlockSpec((2 * RB, H), lambda i, w: (i, 0)),
                pl.BlockSpec((1, H), lambda i, w: (0, 0)),
            ],
        ),
        out_shape=[
            jax.ShapeDtypeStruct((F, H), jnp.float32),
            jax.ShapeDtypeStruct((F, H), jnp.float32),
            jax.ShapeDtypeStruct((1, H), jnp.float32),
        ],
        compiler_params=pltpu.CompilerParams(vmem_limit_bytes=12 << 20),
        name="unpack",
    )(core, full.reshape(8, 8, RBP, 128), theirs.reshape(8, 8, RBP, 128))


def sum_over_devices(kept, given, core):
    kept = kept.reshape(CHIP_COUNT, RBP, 128)
    received = lax.ppermute(given.reshape(CHIP_COUNT, RBP, 128), "core", SWAP)
    chip = (kept.astype(jnp.float32) + received.astype(jnp.float32)).astype(jnp.bfloat16)
    parts = exchange(chip, CHIPS)
    mine = jnp.sum(parts.astype(jnp.float32), axis=0).astype(jnp.bfloat16)
    full = exchange(jnp.broadcast_to(mine[None], (CHIP_COUNT, RBP, 128)), CHIPS)
    theirs = lax.ppermute(full, "core", SWAP)
    grad_self, grad_neigh, grad_bias = unpack(core, full, theirs)
    return grad_self, grad_neigh, grad_bias.reshape(H)


def local(
    node_codes, node_scales, target_rows, owners, local_blocks, neighbours,
    weight_self, weight_neigh, bias, cotangent,
):
    core = lax.axis_index("core")
    owner = owners[:, 0]
    owner_core = (owner // 16) % 2
    owner_chip = (owner // 32) * 16 + owner % 16
    serving = (jnp.arange(R_DEV, dtype=jnp.int32) // RQ) % 2
    place = (owner_core != serving).astype(jnp.int32) * TABLE + owner_chip * NB_DEV + local_blocks
    place = place * SLOT
    asked = jnp.broadcast_to(place.reshape(1, 2, 1, RQ), (4, 2, 16, RQ)).reshape(DEVICES, RQ)
    wanted = exchange(asked, ALL)

    stripes = make_stripes(node_codes, node_scales.astype(jnp.float32))
    own = exchange(stripes.reshape(CHIP_COUNT, NB_DEV, HALF), CHIPS)
    own = own.reshape(TABLE, HALF)
    sister = lax.ppermute(own, "core", SWAP)
    got = exchange(gather(wanted, own, sister), ALL)

    self_codes = select_rows(target_rows, NODE_DEV, node_codes)
    self_scales = select_rows(target_rows, NODE_DEV, node_scales[:, None])
    x_self = (self_codes.astype(jnp.float32) * self_scales.astype(jnp.float32)).astype(jnp.bfloat16)
    pre_self = jnp.dot(x_self, weight_self, preferred_element_type=jnp.float32) + bias
    block, row = neighbours // BR, neighbours % BR
    column = (row // 8) * 1024 + (block // RQ) * 512 + (row % 8) * RQ + block % RQ
    ids = jnp.arange(R_DEV * BR, dtype=jnp.int32)
    tally = jnp.zeros((TGT, R_DEV * BR), jnp.float32)
    for step in range(K):
        tally = tally + (column[:, step][:, None] == ids[None, :]).astype(jnp.float32)

    which = core.reshape(1).astype(jnp.int32)
    hidden, kept, given = layer(
        which, got, tally.astype(jnp.bfloat16), pre_self, x_self.T, weight_neigh, cotangent
    )
    return (hidden,) + sum_over_devices(kept, given, which)


def solution(mesh):
    fine = Mesh(mesh.devices.reshape(4, 2, 4, 4), ALL)
    placed = (
        P(ALL, None),
        P(ALL),
        P(ALL),
        P(ALL, None),
        P(ALL),
        P(ALL, None),
        P(),
        P(),
        P(),
        P(ALL, None),
    )
    return jax.shard_map(
        local,
        mesh=fine,
        in_specs=placed,
        out_specs=(P(ALL, None), P(), P(), P()),
        check_vma=False,
    )
```

```python
import jax
import jax.numpy as jnp
from jax import lax
from jax.experimental import pallas as pl
from jax.experimental.pallas import tpu as pltpu
from jax.sharding import Mesh, PartitionSpec as P

F = 768
H = 1024
BR = 32
K = 10
NODE_DEV = 2048
TGT = 1024
NB_DEV = 64
R_DEV = 128
CHIP_COUNT = 64
DEVICES = 128
HALF = F // 2
RQ = R_DEV // 2
ALL = ("z", "core", "x", "y")
CHIPS = ("z", "x", "y")
SWAP = [(0, 1), (1, 0)]
HB = 256
RB = 96
RBP = 104


def exchange(array, axes):
    return lax.all_to_all(array, axes, split_axis=0, concat_axis=0, tiled=True)


def stripe_copy(codes_ref, codes, sem, k):
    lanes = pl.ds(pl.multiple_of(k * 128, 128), 128)
    return pltpu.make_async_copy(codes_ref.at[:, lanes], codes.at[k], sem.at[k])


def stripe_kernel(codes_ref, scales_ref, stripes_ref, codes, scales, wide, sem):
    k = pl.program_id(0)

    @pl.when(k == 0)
    def _():
        for n in range(6):
            stripe_copy(codes_ref, codes, sem, n).start()
        columns = scales_ref[...].T
        for c in range(NODE_DEV // 128):
            scales[c * 128 : (c + 1) * 128, :] = jnp.broadcast_to(columns[:, c : c + 1], (128, 128))

    stripe_copy(codes_ref, codes, sem, k).wait()
    wide[...] = codes[k].astype(jnp.float32) * scales[...]
    for row in range(BR):
        stripes_ref[row, 0] = wide[pl.ds(row, NB_DEV, stride=BR), :].astype(jnp.bfloat16)


def make_stripes(codes, scales):
    return pl.pallas_call(
        stripe_kernel,
        grid=(6,),
        in_specs=[
            pl.BlockSpec(memory_space=pl.ANY),
            pl.BlockSpec((NODE_DEV // 128, 128), lambda k: (0, 0)),
        ],
        out_specs=pl.BlockSpec((BR, 1, NB_DEV, 128), lambda k: (0, k // 3, 0, k % 3)),
        out_shape=jax.ShapeDtypeStruct((BR, 2, NB_DEV, HALF), jnp.bfloat16),
        scratch_shapes=[
            pltpu.VMEM((6, NODE_DEV, 128), jnp.bfloat16),
            pltpu.VMEM((NODE_DEV, 128), jnp.float32),
            pltpu.VMEM((NODE_DEV, 128), jnp.float32),
            pltpu.SemaphoreType.DMA((6,)),
        ],
        compiler_params=pltpu.CompilerParams(vmem_limit_bytes=60 << 20),
        name="make_stripes",
    )(codes, scales.reshape(NODE_DEV // 128, 128))


GROUP = 16
TABLE = CHIP_COUNT * NB_DEV
SLOT = 4


def gather_kernel(wanted_ref, own_ref, sister_ref, out_ref, table, picked):
    @pl.when(pl.program_id(0) == 0)
    def _():
        for part, source in enumerate((own_ref, sister_ref)):
            for k in range(3):
                table[pl.ds(part * TABLE * SLOT + k, TABLE, stride=SLOT), :] = source[
                    :, k * 128 : (k + 1) * 128
                ].astype(jnp.float32)

    first = pl.program_id(0) * GROUP

    def pair(step, carry):
        for u in range(2):
            base = u * RQ * SLOT
            for j in range(RQ):
                at = pl.multiple_of(wanted_ref[first + 2 * step + u, j], SLOT)
                picked[pl.ds(base + j * SLOT, SLOT), :] = table[pl.ds(at, SLOT), :]
            for k in range(3):
                out_ref[2 * step + u, :, k * 128 : (k + 1) * 128] = picked[
                    pl.ds(base + k, RQ, stride=SLOT), :
                ].astype(jnp.bfloat16)
        return carry

    lax.fori_loop(0, GROUP // 2, pair, 0)


def gather(wanted, own, sister):
    return pl.pallas_call(
        gather_kernel,
        grid_spec=pltpu.PrefetchScalarGridSpec(
            num_scalar_prefetch=1,
            grid=(DEVICES // GROUP,),
            in_specs=[
                pl.BlockSpec((TABLE, HALF), lambda i, w: (0, 0), pipeline_mode=pl.Buffered(1)),
                pl.BlockSpec((TABLE, HALF), lambda i, w: (0, 0), pipeline_mode=pl.Buffered(1)),
            ],
            out_specs=pl.BlockSpec((GROUP, RQ, HALF), lambda i, w: (i, 0, 0)),
            scratch_shapes=[
                pltpu.VMEM((2 * TABLE * SLOT, 128), jnp.float32),
                pltpu.VMEM((2 * RQ * SLOT, 128), jnp.float32),
            ],
        ),
        out_shape=pltpu.HBM((DEVICES, RQ, HALF), jnp.bfloat16),
        compiler_params=pltpu.CompilerParams(vmem_limit_bytes=27 << 20),
        name="gather_rows",
    )(wanted, own, sister)


SIDE = 128


def side_kernel(
    target_ref, column_ref, codes_ref, scales_ref, weight_ref, bias_ref, x_t_ref, pre_ref, tally_ref
):
    hit = target_ref[...] == lax.broadcasted_iota(jnp.int32, (SIDE, NODE_DEV), 1)
    picker = hit.astype(jnp.float32).astype(jnp.bfloat16)
    own_codes = jnp.dot(picker, codes_ref[...], preferred_element_type=jnp.float32)
    own_scales = jnp.sum(jnp.where(hit, scales_ref[...], 0.0), axis=1, keepdims=True)
    x_self = (own_codes * own_scales).astype(jnp.bfloat16)
    x_t_ref[...] = x_self.T
    pre_ref[...] = bias_ref[...] + jnp.dot(
        x_self, weight_ref[...], preferred_element_type=jnp.float32
    )
    wide = 256

    def count(c, carry):
        first = pl.multiple_of(c * wide, wide)
        ids = lax.broadcasted_iota(jnp.int32, (SIDE, wide), 1) + first
        total = jnp.zeros((SIDE, wide), jnp.float32)
        for k in range(K):
            total = total + jnp.where(column_ref[:, k : k + 1] == ids, 1.0, 0.0)
        tally_ref[:, pl.ds(first, wide)] = total.astype(jnp.bfloat16)
        return carry

    lax.fori_loop(0, R_DEV * BR // wide, count, 0)


def side(targets, columns, codes, scales, weight, bias):
    same = lambda i: (0, 0)
    return pl.pallas_call(
        side_kernel,
        grid=(TGT // SIDE,),
        in_specs=[
            pl.BlockSpec((SIDE, 1), lambda i: (i, 0)),
            pl.BlockSpec((SIDE, K), lambda i: (i, 0)),
            pl.BlockSpec((NODE_DEV, F), same),
            pl.BlockSpec((1, NODE_DEV), same),
            pl.BlockSpec((F, H), same),
            pl.BlockSpec((1, H), same),
        ],
        out_specs=[
            pl.BlockSpec((F, SIDE), lambda i: (0, i)),
            pl.BlockSpec((SIDE, H), lambda i: (i, 0)),
            pl.BlockSpec((SIDE, R_DEV * BR), lambda i: (i, 0)),
        ],
        out_shape=[
            jax.ShapeDtypeStruct((F, TGT), jnp.bfloat16),
            jax.ShapeDtypeStruct((TGT, H), jnp.float32),
            jax.ShapeDtypeStruct((TGT, R_DEV * BR), jnp.bfloat16),
        ],
        compiler_params=pltpu.CompilerParams(vmem_limit_bytes=24 << 20),
        name="side",
    )(targets[:, None], columns, codes, scales[None, :], weight, bias[None, :])


MEAN_STEPS = 4
COLS = 2 * BR * R_DEV // 2 // MEAN_STEPS


def layer_kernel(
    core_ref, got_ref, tally_ref, pre_ref, x_t_ref, weight_ref, cot_ref,
    hidden_ref, kept_ref, given_ref, acc, mean, mean_t,
):
    step = pl.program_id(0)

    @pl.when(step < MEAN_STEPS)
    def _():
        rows = jnp.concatenate(
            [
                jnp.concatenate([got_ref[2 * e + half] for e in range(COLS // RQ)], axis=0)
                for half in range(2)
            ],
            axis=1,
        )
        part = jnp.dot(tally_ref[...], rows, preferred_element_type=jnp.float32)

        @pl.when(step == 0)
        def _():
            acc[...] = part

        @pl.when(step > 0)
        def _():
            acc[...] += part

    @pl.when(step == MEAN_STEPS - 1)
    def _():
        value = (acc[...] / K).astype(jnp.bfloat16)
        mean[...] = value
        mean_t[...] = value.T

    @pl.when(step >= MEAN_STEPS)
    def _():
        pre = pre_ref[...] + jnp.dot(
            mean[...], weight_ref[...], preferred_element_type=jnp.float32
        )
        square = pre * pre
        tangent = jnp.tanh(0.7978845608 * (pre + 0.044715 * pre * square))
        rest = 1.0 + tangent
        hidden_ref[...] = (0.5 * pre * rest).astype(jnp.bfloat16)
        slope = 0.5 * rest + 0.5 * pre * (1.0 - tangent * tangent) * 0.7978845608 * (
            1.0 + 3.0 * 0.044715 * square
        )
        wide = cot_ref[...].astype(jnp.float32) * slope
        delta = wide.astype(jnp.bfloat16)
        bias_term = jnp.sum(delta.astype(jnp.float32), axis=0, keepdims=True)
        first = core_ref[0] == 0
        grad_self = jnp.dot(x_t_ref[...], delta, preferred_element_type=jnp.float32)
        grad_neigh = jnp.dot(mean_t[...], delta, preferred_element_type=jnp.float32)
        tail = jnp.broadcast_to(bias_term, (RBP - RB, HB))
        for ref, value in (
            (kept_ref, jnp.where(first, grad_self, grad_neigh)),
            (given_ref, jnp.where(first, grad_neigh, grad_self)),
        ):
            for c in range(HB // 128):
                lanes = slice(c * 128, (c + 1) * 128)
                for r in range(8):
                    ref[r, c] = jnp.concatenate(
                        [value[r * RB : (r + 1) * RB, lanes], tail[:, lanes]], axis=0
                    ).astype(jnp.bfloat16)


def layer(core, got, tally, pre_self, x_t, weight_neigh, cotangent):
    last = MEAN_STEPS - 1
    early = lambda i, w: jnp.minimum(i, last)
    late = lambda i, w: jnp.maximum(i - MEAN_STEPS, 0)
    term = pl.BlockSpec((8, HB // 128, RBP, 128), lambda i, w: (0, late(i, w), 0, 0))
    return pl.pallas_call(
        layer_kernel,
        grid_spec=pltpu.PrefetchScalarGridSpec(
            num_scalar_prefetch=1,
            grid=(MEAN_STEPS + H // HB,),
            in_specs=[
                pl.BlockSpec((DEVICES // MEAN_STEPS, RQ, HALF), lambda i, w: (early(i, w), 0, 0)),
                pl.BlockSpec((TGT, COLS), lambda i, w: (0, early(i, w))),
                pl.BlockSpec((TGT, HB), lambda i, w: (0, late(i, w))),
                pl.BlockSpec((F, TGT), lambda i, w: (0, 0)),
                pl.BlockSpec((F, HB), lambda i, w: (0, late(i, w))),
                pl.BlockSpec((TGT, HB), lambda i, w: (0, late(i, w))),
            ],
            out_specs=[pl.BlockSpec((TGT, HB), lambda i, w: (0, late(i, w))), term, term],
            scratch_shapes=[
                pltpu.VMEM((TGT, F), jnp.float32),
                pltpu.VMEM((TGT, F), jnp.bfloat16),
                pltpu.VMEM((F, TGT), jnp.bfloat16),
            ],
        ),
        out_shape=[
            jax.ShapeDtypeStruct((TGT, H), jnp.bfloat16),
            jax.ShapeDtypeStruct((8, 8, RBP, 128), jnp.bfloat16),
            jax.ShapeDtypeStruct((8, 8, RBP, 128), jnp.bfloat16),
        ],
        compiler_params=pltpu.CompilerParams(vmem_limit_bytes=28 << 20),
        name="layer",
    )(core, got, tally, pre_self, x_t, weight_neigh, cotangent)


def unpack_kernel(core_ref, full_ref, theirs_ref, self_ref, neigh_ref, bias_ref):
    first = core_ref[0] == 0
    for r in range(2):
        rows = slice(r * RB, (r + 1) * RB)
        for c in range(8):
            lanes = slice(c * 128, (c + 1) * 128)
            a = full_ref[r, c].astype(jnp.float32)
            b = theirs_ref[r, c].astype(jnp.float32)
            self_ref[rows, lanes] = jnp.where(first, a[:RB], b[:RB])
            neigh_ref[rows, lanes] = jnp.where(first, b[:RB], a[:RB])
            bias_ref[:, lanes] = a[RB : RB + 1]


def unpack(core, full, theirs):
    chunks = pl.BlockSpec((2, 8, RBP, 128), lambda i, w: (i, 0, 0, 0))
    return pl.pallas_call(
        unpack_kernel,
        grid_spec=pltpu.PrefetchScalarGridSpec(
            num_scalar_prefetch=1,
            grid=(4,),
            in_specs=[chunks, chunks],
            out_specs=[
                pl.BlockSpec((2 * RB, H), lambda i, w: (i, 0)),
                pl.BlockSpec((2 * RB, H), lambda i, w: (i, 0)),
                pl.BlockSpec((1, H), lambda i, w: (0, 0)),
            ],
        ),
        out_shape=[
            jax.ShapeDtypeStruct((F, H), jnp.float32),
            jax.ShapeDtypeStruct((F, H), jnp.float32),
            jax.ShapeDtypeStruct((1, H), jnp.float32),
        ],
        compiler_params=pltpu.CompilerParams(vmem_limit_bytes=12 << 20),
        name="unpack",
    )(core, full.reshape(8, 8, RBP, 128), theirs.reshape(8, 8, RBP, 128))


def sum_over_devices(kept, given, core):
    kept = kept.reshape(CHIP_COUNT, RBP, 128)
    received = lax.ppermute(given.reshape(CHIP_COUNT, RBP, 128), "core", SWAP)
    chip = (kept.astype(jnp.float32) + received.astype(jnp.float32)).astype(jnp.bfloat16)
    parts = exchange(chip, CHIPS)
    mine = jnp.sum(parts.astype(jnp.float32), axis=0).astype(jnp.bfloat16)
    full = exchange(jnp.broadcast_to(mine[None], (CHIP_COUNT, RBP, 128)), CHIPS)
    theirs = lax.ppermute(full, "core", SWAP)
    grad_self, grad_neigh, grad_bias = unpack(core, full, theirs)
    return grad_self, grad_neigh, grad_bias.reshape(H)


def local(
    node_codes, node_scales, target_rows, owners, local_blocks, neighbours,
    weight_self, weight_neigh, bias, cotangent,
):
    core = lax.axis_index("core")
    owner = owners[:, 0]
    owner_core = (owner // 16) % 2
    owner_chip = (owner // 32) * 16 + owner % 16
    serving = (jnp.arange(R_DEV, dtype=jnp.int32) // RQ) % 2
    place = (owner_core != serving).astype(jnp.int32) * TABLE + owner_chip * NB_DEV + local_blocks
    place = place * SLOT
    asked = jnp.broadcast_to(place.reshape(1, 2, 1, RQ), (4, 2, 16, RQ)).reshape(DEVICES, RQ)
    wanted = exchange(asked, ALL)

    stripes = make_stripes(node_codes, node_scales.astype(jnp.float32))
    own = exchange(stripes.reshape(CHIP_COUNT, NB_DEV, HALF), CHIPS)
    own = own.reshape(TABLE, HALF)
    sister = lax.ppermute(own, "core", SWAP)
    send = gather(wanted, own, sister)
    send, neighbours, target_rows = lax.optimization_barrier((send, neighbours, target_rows))
    got = exchange(send, ALL)

    block, row = neighbours // BR, neighbours % BR
    column = (row // 8) * 1024 + (block // RQ) * 512 + (row % 8) * RQ + block % RQ
    x_t, pre_self, tally = side(
        target_rows, column, node_codes, node_scales.astype(jnp.float32), weight_self, bias
    )
    which = core.reshape(1).astype(jnp.int32)
    hidden, kept, given = layer(
        which, got, tally, pre_self, x_t, weight_neigh, cotangent
    )
    return (hidden,) + sum_over_devices(kept, given, which)


def solution(mesh):
    fine = Mesh(mesh.devices.reshape(4, 2, 4, 4), ALL)
    placed = (
        P(ALL, None),
        P(ALL),
        P(ALL),
        P(ALL, None),
        P(ALL),
        P(ALL, None),
        P(),
        P(),
        P(),
        P(ALL, None),
    )
    return jax.shard_map(
        local,
        mesh=fine,
        in_specs=placed,
        out_specs=(P(ALL, None), P(), P(), P()),
        check_vma=False,
    )
```

```python
import jax
import jax.numpy as jnp
from jax import lax
from jax.experimental import pallas as pl
from jax.experimental.pallas import tpu as pltpu
from jax.sharding import Mesh, PartitionSpec as P

F = 768
H = 1024
BR = 32
K = 10
NODE_DEV = 2048
TGT = 1024
NB_DEV = 64
R_DEV = 128
CHIP_COUNT = 64
DEVICES = 128
HALF = F // 2
RQ = R_DEV // 2
ALL = ("z", "core", "x", "y")
CHIPS = ("z", "x", "y")
SWAP = [(0, 1), (1, 0)]
HB = 256
RB = 96
RBP = 104


def exchange(array, axes):
    return lax.all_to_all(array, axes, split_axis=0, concat_axis=0, tiled=True)


def stripe_copy(codes_ref, codes, sem, k):
    lanes = pl.ds(pl.multiple_of(k * 128, 128), 128)
    return pltpu.make_async_copy(codes_ref.at[:, lanes], codes.at[k], sem.at[k])


def stripe_kernel(codes_ref, scales_ref, stripes_ref, codes, scales, wide, sem):
    k = pl.program_id(0)

    @pl.when(k == 0)
    def _():
        for n in range(6):
            stripe_copy(codes_ref, codes, sem, n).start()
        columns = scales_ref[...].T
        for c in range(NODE_DEV // 128):
            scales[c * 128 : (c + 1) * 128, :] = jnp.broadcast_to(columns[:, c : c + 1], (128, 128))

    stripe_copy(codes_ref, codes, sem, k).wait()
    wide[...] = codes[k].astype(jnp.float32) * scales[...]
    for row in range(BR):
        stripes_ref[row, 0] = wide[pl.ds(row, NB_DEV, stride=BR), :].astype(jnp.bfloat16)


def make_stripes(codes, scales):
    return pl.pallas_call(
        stripe_kernel,
        grid=(6,),
        in_specs=[
            pl.BlockSpec(memory_space=pl.ANY),
            pl.BlockSpec((NODE_DEV // 128, 128), lambda k: (0, 0)),
        ],
        out_specs=pl.BlockSpec((BR, 1, NB_DEV, 128), lambda k: (0, k // 3, 0, k % 3)),
        out_shape=jax.ShapeDtypeStruct((BR, 2, NB_DEV, HALF), jnp.bfloat16),
        scratch_shapes=[
            pltpu.VMEM((6, NODE_DEV, 128), jnp.bfloat16),
            pltpu.VMEM((NODE_DEV, 128), jnp.float32),
            pltpu.VMEM((NODE_DEV, 128), jnp.float32),
            pltpu.SemaphoreType.DMA((6,)),
        ],
        compiler_params=pltpu.CompilerParams(vmem_limit_bytes=60 << 20),
        name="make_stripes",
    )(codes, scales.reshape(NODE_DEV // 128, 128))


GROUP = 16
TABLE = CHIP_COUNT * NB_DEV
SLOT = 4


STAGES = 8
STAGE = 2 * TABLE // STAGES


def gather_kernel(wanted_ref, own_ref, sister_ref, out_ref, table, picked, narrow, sem):
    @pl.when(pl.program_id(0) == 0)
    def _():
        copies = []
        for n in range(STAGES):
            source = own_ref if n < STAGES // 2 else sister_ref
            start = n % (STAGES // 2) * STAGE
            copies.append(
                pltpu.make_async_copy(source.at[pl.ds(start, STAGE)], narrow.at[n], sem.at[n])
            )
            copies[-1].start()
        for n in range(STAGES):
            copies[n].wait()
            for k in range(3):
                table[pl.ds(n * STAGE * SLOT + k, STAGE, stride=SLOT), :] = narrow[
                    n, :, k * 128 : (k + 1) * 128
                ].astype(jnp.float32)

    first = pl.program_id(0) * GROUP

    def pair(step, carry):
        for u in range(2):
            base = u * RQ * SLOT
            for j in range(RQ):
                at = pl.multiple_of(wanted_ref[first + 2 * step + u, j], SLOT)
                picked[pl.ds(base + j * SLOT, SLOT), :] = table[pl.ds(at, SLOT), :]
            for k in range(3):
                out_ref[2 * step + u, :, k * 128 : (k + 1) * 128] = picked[
                    pl.ds(base + k, RQ, stride=SLOT), :
                ].astype(jnp.bfloat16)
        return carry

    lax.fori_loop(0, GROUP // 2, pair, 0)


def gather(wanted, own, sister):
    return pl.pallas_call(
        gather_kernel,
        grid_spec=pltpu.PrefetchScalarGridSpec(
            num_scalar_prefetch=1,
            grid=(DEVICES // GROUP,),
            in_specs=[
                pl.BlockSpec(memory_space=pl.ANY),
                pl.BlockSpec(memory_space=pl.ANY),
            ],
            out_specs=pl.BlockSpec((GROUP, RQ, HALF), lambda i, w: (i, 0, 0)),
            scratch_shapes=[
                pltpu.VMEM((2 * TABLE * SLOT, 128), jnp.float32),
                pltpu.VMEM((2 * RQ * SLOT, 128), jnp.float32),
                pltpu.VMEM((STAGES, STAGE, HALF), jnp.bfloat16),
                pltpu.SemaphoreType.DMA((STAGES,)),
            ],
        ),
        out_shape=pltpu.HBM((DEVICES, RQ, HALF), jnp.bfloat16),
        compiler_params=pltpu.CompilerParams(vmem_limit_bytes=27 << 20),
        name="gather_rows",
    )(wanted, own, sister)


SIDE = 128


def side_kernel(
    target_ref, column_ref, codes_ref, scales_ref, weight_ref, bias_ref, x_t_ref, pre_ref, tally_ref
):
    hit = target_ref[...] == lax.broadcasted_iota(jnp.int32, (SIDE, NODE_DEV), 1)
    picker = hit.astype(jnp.float32).astype(jnp.bfloat16)
    own_codes = jnp.dot(picker, codes_ref[...], preferred_element_type=jnp.float32)
    own_scales = jnp.sum(jnp.where(hit, scales_ref[...], 0.0), axis=1, keepdims=True)
    x_self = (own_codes * own_scales).astype(jnp.bfloat16)
    x_t_ref[...] = x_self.T
    pre_ref[...] = bias_ref[...] + jnp.dot(
        x_self, weight_ref[...], preferred_element_type=jnp.float32
    )
    wide = 256

    def count(c, carry):
        first = pl.multiple_of(c * wide, wide)
        ids = lax.broadcasted_iota(jnp.int32, (SIDE, wide), 1) + first
        total = jnp.zeros((SIDE, wide), jnp.float32)
        for k in range(K):
            total = total + jnp.where(column_ref[:, k : k + 1] == ids, 1.0, 0.0)
        tally_ref[:, pl.ds(first, wide)] = total.astype(jnp.bfloat16)
        return carry

    lax.fori_loop(0, R_DEV * BR // wide, count, 0)


def side(targets, columns, codes, scales, weight, bias):
    same = lambda i: (0, 0)
    return pl.pallas_call(
        side_kernel,
        grid=(TGT // SIDE,),
        in_specs=[
            pl.BlockSpec((SIDE, 1), lambda i: (i, 0)),
            pl.BlockSpec((SIDE, K), lambda i: (i, 0)),
            pl.BlockSpec((NODE_DEV, F), same),
            pl.BlockSpec((1, NODE_DEV), same),
            pl.BlockSpec((F, H), same),
            pl.BlockSpec((1, H), same),
        ],
        out_specs=[
            pl.BlockSpec((F, SIDE), lambda i: (0, i)),
            pl.BlockSpec((SIDE, H), lambda i: (i, 0)),
            pl.BlockSpec((SIDE, R_DEV * BR), lambda i: (i, 0)),
        ],
        out_shape=[
            jax.ShapeDtypeStruct((F, TGT), jnp.bfloat16),
            jax.ShapeDtypeStruct((TGT, H), jnp.float32),
            jax.ShapeDtypeStruct((TGT, R_DEV * BR), jnp.bfloat16),
        ],
        compiler_params=pltpu.CompilerParams(vmem_limit_bytes=24 << 20),
        name="side",
    )(targets[:, None], columns, codes, scales[None, :], weight, bias[None, :])


MEAN_STEPS = 4
COLS = R_DEV * BR // MEAN_STEPS
PIECES = DEVICES // MEAN_STEPS
LATE = H // HB


def layer_kernel(
    core_ref, got_ref, tally_ref, pre_ref, x_t_ref, weight_ref, cot_ref,
    hidden_ref, kept_ref, given_ref,
    got, tally, pre_self, x_t, weight, cot, hidden, kept, given, acc, mean, mean_t, sem, out_sem,
):
    count = 0

    def fetch(source, target):
        nonlocal count
        copy = pltpu.make_async_copy(source, target, sem.at[count])
        count += 1
        copy.start()
        return copy

    early = []
    for n in range(MEAN_STEPS):
        early.append(
            (
                fetch(got_ref.at[pl.ds(n * PIECES, PIECES)], got.at[n]),
                fetch(tally_ref.at[:, pl.ds(n * COLS, COLS)], tally.at[n]),
            )
        )
    late = [
        fetch(source, target)
        for source, target in (
            (weight_ref, weight), (pre_ref, pre_self), (cot_ref, cot), (x_t_ref, x_t)
        )
    ]
    for n in range(MEAN_STEPS):
        for copy in early[n]:
            copy.wait()
        rows = jnp.concatenate(
            [
                jnp.concatenate([got[n, 2 * e + half] for e in range(COLS // RQ)], axis=0)
                for half in range(2)
            ],
            axis=1,
        )
        part = jnp.dot(tally[n], rows, preferred_element_type=jnp.float32)
        if n == 0:
            acc[...] = part
        elif n < MEAN_STEPS - 1:
            acc[...] += part
        else:
            value = ((acc[...] + part) / K).astype(jnp.bfloat16)
            mean[...] = value
            mean_t[...] = value.T
    for copy in late:
        copy.wait()
    first = core_ref[0] == 0
    leaving = []
    for n in range(LATE):
        block = slice(n * HB, (n + 1) * HB)
        pre = pre_self[:, block] + jnp.dot(
            mean[...], weight[:, block], preferred_element_type=jnp.float32
        )
        square = pre * pre
        tangent = jnp.tanh(0.7978845608 * (pre + 0.044715 * pre * square))
        rest = 1.0 + tangent
        hidden[:, block] = (0.5 * pre * rest).astype(jnp.bfloat16)
        slope = 0.5 * rest + 0.5 * pre * (1.0 - tangent * tangent) * 0.7978845608 * (
            1.0 + 3.0 * 0.044715 * square
        )
        delta = (cot[:, block].astype(jnp.float32) * slope).astype(jnp.bfloat16)
        bias_term = jnp.sum(delta.astype(jnp.float32), axis=0, keepdims=True)
        grad_self = jnp.dot(x_t[...], delta, preferred_element_type=jnp.float32)
        grad_neigh = jnp.dot(mean_t[...], delta, preferred_element_type=jnp.float32)
        tail = jnp.broadcast_to(bias_term, (RBP - RB, HB))
        for ref, value in (
            (given, jnp.where(first, grad_neigh, grad_self)),
            (kept, jnp.where(first, grad_self, grad_neigh)),
        ):
            for c in range(HB // 128):
                lanes = slice(c * 128, (c + 1) * 128)
                for r in range(8):
                    ref[n, r, c] = jnp.concatenate(
                        [value[r * RB : (r + 1) * RB, lanes], tail[:, lanes]], axis=0
                    ).astype(jnp.bfloat16)
        chunk = pl.ds(n * (HB // 128), HB // 128)
        for e, (source, target) in enumerate(
            (
                (given.at[n], given_ref.at[:, chunk]),
                (kept.at[n], kept_ref.at[:, chunk]),
                (hidden.at[:, pl.ds(n * HB, HB)], hidden_ref.at[:, pl.ds(n * HB, HB)]),
            )
        ):
            copy = pltpu.make_async_copy(source, target, out_sem.at[3 * n + e])
            copy.start()
            leaving.append(copy)
    for copy in leaving:
        copy.wait()


def layer(core, got, tally, pre_self, x_t, weight_neigh, cotangent):
    whole = pl.BlockSpec(memory_space=pl.ANY)
    return pl.pallas_call(
        layer_kernel,
        in_specs=[pl.BlockSpec(memory_space=pltpu.SMEM)] + [whole] * 6,
        out_specs=[whole] * 3,
        out_shape=[
            jax.ShapeDtypeStruct((TGT, H), jnp.bfloat16),
            jax.ShapeDtypeStruct((8, 8, RBP, 128), jnp.bfloat16),
            jax.ShapeDtypeStruct((8, 8, RBP, 128), jnp.bfloat16),
        ],
        scratch_shapes=[
            pltpu.VMEM((MEAN_STEPS, PIECES, RQ, HALF), jnp.bfloat16),
            pltpu.VMEM((MEAN_STEPS, TGT, COLS), jnp.bfloat16),
            pltpu.VMEM((TGT, H), jnp.float32),
            pltpu.VMEM((F, TGT), jnp.bfloat16),
            pltpu.VMEM((F, H), jnp.bfloat16),
            pltpu.VMEM((TGT, H), jnp.bfloat16),
            pltpu.VMEM((TGT, H), jnp.bfloat16),
            pltpu.VMEM((LATE, 8, HB // 128, RBP, 128), jnp.bfloat16),
            pltpu.VMEM((LATE, 8, HB // 128, RBP, 128), jnp.bfloat16),
            pltpu.VMEM((TGT, F), jnp.float32),
            pltpu.VMEM((TGT, F), jnp.bfloat16),
            pltpu.VMEM((F, TGT), jnp.bfloat16),
            pltpu.SemaphoreType.DMA((2 * MEAN_STEPS + 4,)),
            pltpu.SemaphoreType.DMA((3 * LATE,)),
        ],
        compiler_params=pltpu.CompilerParams(vmem_limit_bytes=58 << 20),
        name="layer",
    )(core, got, tally, pre_self, x_t, weight_neigh, cotangent)


def unpack_kernel(core_ref, full_ref, theirs_ref, self_ref, neigh_ref, bias_ref):
    first = core_ref[0] == 0
    for r in range(2):
        rows = slice(r * RB, (r + 1) * RB)
        for c in range(8):
            lanes = slice(c * 128, (c + 1) * 128)
            a = full_ref[r, c].astype(jnp.float32)
            b = theirs_ref[r, c].astype(jnp.float32)
            self_ref[rows, lanes] = jnp.where(first, a[:RB], b[:RB])
            neigh_ref[rows, lanes] = jnp.where(first, b[:RB], a[:RB])
            bias_ref[:, lanes] = a[RB : RB + 1]


def unpack(core, full, theirs):
    chunks = pl.BlockSpec((2, 8, RBP, 128), lambda i, w: (i, 0, 0, 0))
    return pl.pallas_call(
        unpack_kernel,
        grid_spec=pltpu.PrefetchScalarGridSpec(
            num_scalar_prefetch=1,
            grid=(4,),
            in_specs=[chunks, chunks],
            out_specs=[
                pl.BlockSpec((2 * RB, H), lambda i, w: (i, 0)),
                pl.BlockSpec((2 * RB, H), lambda i, w: (i, 0)),
                pl.BlockSpec((1, H), lambda i, w: (0, 0)),
            ],
        ),
        out_shape=[
            jax.ShapeDtypeStruct((F, H), jnp.float32),
            jax.ShapeDtypeStruct((F, H), jnp.float32),
            jax.ShapeDtypeStruct((1, H), jnp.float32),
        ],
        compiler_params=pltpu.CompilerParams(vmem_limit_bytes=12 << 20),
        name="unpack",
    )(core, full.reshape(8, 8, RBP, 128), theirs.reshape(8, 8, RBP, 128))


def sum_over_devices(kept, given, core):
    kept = kept.reshape(CHIP_COUNT, RBP, 128)
    received = lax.ppermute(given.reshape(CHIP_COUNT, RBP, 128), "core", SWAP)
    chip = (kept.astype(jnp.float32) + received.astype(jnp.float32)).astype(jnp.bfloat16)
    parts = exchange(chip, CHIPS)
    mine = jnp.sum(parts.astype(jnp.float32), axis=0).astype(jnp.bfloat16)
    full = exchange(jnp.broadcast_to(mine[None], (CHIP_COUNT, RBP, 128)), CHIPS)
    theirs = lax.ppermute(full, "core", SWAP)
    grad_self, grad_neigh, grad_bias = unpack(core, full, theirs)
    return grad_self, grad_neigh, grad_bias.reshape(H)


def local(
    node_codes, node_scales, target_rows, owners, local_blocks, neighbours,
    weight_self, weight_neigh, bias, cotangent,
):
    core = lax.axis_index("core")
    owner = owners[:, 0]
    owner_core = (owner // 16) % 2
    owner_chip = (owner // 32) * 16 + owner % 16
    serving = (jnp.arange(R_DEV, dtype=jnp.int32) // RQ) % 2
    place = (owner_core != serving).astype(jnp.int32) * TABLE + owner_chip * NB_DEV + local_blocks
    place = place * SLOT
    asked = jnp.broadcast_to(place.reshape(1, 2, 1, RQ), (4, 2, 16, RQ)).reshape(DEVICES, RQ)
    wanted = exchange(asked, ALL)

    stripes = make_stripes(node_codes, node_scales.astype(jnp.float32))
    own = exchange(stripes.reshape(CHIP_COUNT, NB_DEV, HALF), CHIPS)
    own = own.reshape(TABLE, HALF)
    sister = lax.ppermute(own, "core", SWAP)
    send = gather(wanted, own, sister)
    send, neighbours, target_rows = lax.optimization_barrier((send, neighbours, target_rows))
    got = exchange(send, ALL)

    block, row = neighbours // BR, neighbours % BR
    column = (row // 8) * 1024 + (block // RQ) * 512 + (row % 8) * RQ + block % RQ
    x_t, pre_self, tally = side(
        target_rows, column, node_codes, node_scales.astype(jnp.float32), weight_self, bias
    )
    which = core.reshape(1).astype(jnp.int32)
    hidden, kept, given = layer(
        which, got, tally, pre_self, x_t, weight_neigh, cotangent
    )
    return (hidden,) + sum_over_devices(kept, given, which)


def solution(mesh):
    fine = Mesh(mesh.devices.reshape(4, 2, 4, 4), ALL)
    placed = (
        P(ALL, None),
        P(ALL),
        P(ALL),
        P(ALL, None),
        P(ALL),
        P(ALL, None),
        P(),
        P(),
        P(),
        P(ALL, None),
    )
    return jax.shard_map(
        local,
        mesh=fine,
        in_specs=placed,
        out_specs=(P(ALL, None), P(), P(), P()),
        check_vma=False,
    )
```

```python
import jax
import jax.numpy as jnp
from jax import lax
from jax.experimental import pallas as pl
from jax.experimental.pallas import tpu as pltpu
from jax.sharding import Mesh, PartitionSpec as P

F = 768
H = 1024
BR = 32
K = 10
NODE_DEV = 2048
TGT = 1024
NB_DEV = 64
R_DEV = 128
CHIP_COUNT = 64
DEVICES = 128
HALF = F // 2
RQ = R_DEV // 2
ALL = ("z", "core", "x", "y")
CHIPS = ("z", "x", "y")
SWAP = [(0, 1), (1, 0)]
HB = 256
RB = 96
RBP = 104


def exchange(array, axes):
    return lax.all_to_all(array, axes, split_axis=0, concat_axis=0, tiled=True)


PITCH = BR + 4


def stripe_copy(codes_ref, codes, sem, k):
    lanes = pl.ds(pl.multiple_of(k * 128, 128), 128)
    return pltpu.make_async_copy(codes_ref.at[:, lanes], codes.at[k], sem.at[k])


def stripe_kernel(codes_ref, scales_ref, stripes_ref, codes, scales, wide, sem):
    k = pl.program_id(0)

    @pl.when(k == 0)
    def _():
        for n in range(6):
            stripe_copy(codes_ref, codes, sem, n).start()
        columns = scales_ref[...].T
        for c in range(NODE_DEV // 128):
            scales[c * 128 : (c + 1) * 128, :] = jnp.broadcast_to(columns[:, c : c + 1], (128, 128))

    stripe_copy(codes_ref, codes, sem, k).wait()
    product = codes[k].astype(jnp.float32) * scales[...]
    for b in range(NB_DEV):
        wide[b * PITCH : b * PITCH + BR, :] = product[b * BR : (b + 1) * BR]
    for row in range(BR):
        stripes_ref[row, 0] = wide[pl.ds(row, NB_DEV, stride=PITCH), :].astype(jnp.bfloat16)


def make_stripes(codes, scales):
    return pl.pallas_call(
        stripe_kernel,
        grid=(6,),
        in_specs=[
            pl.BlockSpec(memory_space=pl.ANY),
            pl.BlockSpec((NODE_DEV // 128, 128), lambda k: (0, 0)),
        ],
        out_specs=pl.BlockSpec((BR, 1, NB_DEV, 128), lambda k: (0, k // 3, 0, k % 3)),
        out_shape=jax.ShapeDtypeStruct((BR, 2, NB_DEV, HALF), jnp.bfloat16),
        scratch_shapes=[
            pltpu.VMEM((6, NODE_DEV, 128), jnp.bfloat16),
            pltpu.VMEM((NODE_DEV, 128), jnp.float32),
            pltpu.VMEM((NB_DEV * PITCH, 128), jnp.float32),
            pltpu.SemaphoreType.DMA((6,)),
        ],
        compiler_params=pltpu.CompilerParams(vmem_limit_bytes=60 << 20),
        name="make_stripes",
    )(codes, scales.reshape(NODE_DEV // 128, 128))


GROUP = 16
TABLE = CHIP_COUNT * NB_DEV
SLOT = 4


STAGES = 8
STAGE = 2 * TABLE // STAGES


def gather_kernel(wanted_ref, own_ref, sister_ref, out_ref, table, picked, narrow, sem):
    @pl.when(pl.program_id(0) == 0)
    def _():
        copies = []
        for n in range(STAGES):
            source = own_ref if n < STAGES // 2 else sister_ref
            start = n % (STAGES // 2) * STAGE
            copies.append(
                pltpu.make_async_copy(source.at[pl.ds(start, STAGE)], narrow.at[n], sem.at[n])
            )
            copies[-1].start()
        for n in range(STAGES):
            copies[n].wait()
            for k in range(3):
                table[pl.ds(n * STAGE * SLOT + k, STAGE, stride=SLOT), :] = narrow[
                    n, :, k * 128 : (k + 1) * 128
                ].astype(jnp.float32)

    first = pl.program_id(0) * GROUP

    def pair(step, carry):
        for u in range(2):
            base = u * RQ * SLOT
            for j in range(RQ):
                at = pl.multiple_of(wanted_ref[first + 2 * step + u, j], SLOT)
                picked[pl.ds(base + j * SLOT, SLOT), :] = table[pl.ds(at, SLOT), :]
            for k in range(3):
                out_ref[2 * step + u, :, k * 128 : (k + 1) * 128] = picked[
                    pl.ds(base + k, RQ, stride=SLOT), :
                ].astype(jnp.bfloat16)
        return carry

    lax.fori_loop(0, GROUP // 2, pair, 0)


def gather(wanted, own, sister):
    return pl.pallas_call(
        gather_kernel,
        grid_spec=pltpu.PrefetchScalarGridSpec(
            num_scalar_prefetch=1,
            grid=(DEVICES // GROUP,),
            in_specs=[
                pl.BlockSpec(memory_space=pl.ANY),
                pl.BlockSpec(memory_space=pl.ANY),
            ],
            out_specs=pl.BlockSpec((GROUP, RQ, HALF), lambda i, w: (i, 0, 0)),
            scratch_shapes=[
                pltpu.VMEM((2 * TABLE * SLOT, 128), jnp.float32),
                pltpu.VMEM((2 * RQ * SLOT, 128), jnp.float32),
                pltpu.VMEM((STAGES, STAGE, HALF), jnp.bfloat16),
                pltpu.SemaphoreType.DMA((STAGES,)),
            ],
        ),
        out_shape=pltpu.HBM((DEVICES, RQ, HALF), jnp.bfloat16),
        compiler_params=pltpu.CompilerParams(vmem_limit_bytes=27 << 20),
        name="gather_rows",
    )(wanted, own, sister)


SIDE = 128


def side_kernel(
    target_ref, column_ref, codes_ref, scales_ref, weight_ref, bias_ref, x_t_ref, pre_ref, tally_ref
):
    hit = target_ref[...] == lax.broadcasted_iota(jnp.int32, (SIDE, NODE_DEV), 1)
    picker = hit.astype(jnp.float32).astype(jnp.bfloat16)
    own_codes = jnp.dot(picker, codes_ref[...], preferred_element_type=jnp.float32)
    own_scales = jnp.sum(jnp.where(hit, scales_ref[...], 0.0), axis=1, keepdims=True)
    x_self = (own_codes * own_scales).astype(jnp.bfloat16)
    x_t_ref[...] = x_self.T
    pre_ref[...] = bias_ref[...] + jnp.dot(
        x_self, weight_ref[...], preferred_element_type=jnp.float32
    )
    wide = 256

    def count(c, carry):
        first = pl.multiple_of(c * wide, wide)
        ids = lax.broadcasted_iota(jnp.int32, (SIDE, wide), 1) + first
        total = jnp.zeros((SIDE, wide), jnp.float32)
        for k in range(K):
            total = total + jnp.where(column_ref[:, k : k + 1] == ids, 1.0, 0.0)
        tally_ref[:, pl.ds(first, wide)] = total.astype(jnp.bfloat16)
        return carry

    lax.fori_loop(0, R_DEV * BR // wide, count, 0)


def side(targets, columns, codes, scales, weight, bias):
    same = lambda i: (0, 0)
    return pl.pallas_call(
        side_kernel,
        grid=(TGT // SIDE,),
        in_specs=[
            pl.BlockSpec((SIDE, 1), lambda i: (i, 0)),
            pl.BlockSpec((SIDE, K), lambda i: (i, 0)),
            pl.BlockSpec((NODE_DEV, F), same),
            pl.BlockSpec((1, NODE_DEV), same),
            pl.BlockSpec((F, H), same),
            pl.BlockSpec((1, H), same),
        ],
        out_specs=[
            pl.BlockSpec((F, SIDE), lambda i: (0, i)),
            pl.BlockSpec((SIDE, H), lambda i: (i, 0)),
            pl.BlockSpec((SIDE, R_DEV * BR), lambda i: (i, 0)),
        ],
        out_shape=[
            jax.ShapeDtypeStruct((F, TGT), jnp.bfloat16),
            jax.ShapeDtypeStruct((TGT, H), jnp.float32),
            jax.ShapeDtypeStruct((TGT, R_DEV * BR), jnp.bfloat16),
        ],
        compiler_params=pltpu.CompilerParams(vmem_limit_bytes=24 << 20),
        name="side",
    )(targets[:, None], columns, codes, scales[None, :], weight, bias[None, :])


MEAN_STEPS = 4
COLS = R_DEV * BR // MEAN_STEPS
PIECES = DEVICES // MEAN_STEPS
LATE = H // HB


def layer_kernel(
    core_ref, got_ref, tally_ref, pre_ref, x_t_ref, weight_ref, cot_ref,
    hidden_ref, kept_ref, given_ref,
    got, tally, pre_self, x_t, weight, cot, hidden, kept, given, acc, mean, mean_t, sem, out_sem,
):
    count = 0

    def fetch(source, target):
        nonlocal count
        copy = pltpu.make_async_copy(source, target, sem.at[count])
        count += 1
        copy.start()
        return copy

    early = []
    for n in range(MEAN_STEPS):
        early.append(
            (
                fetch(got_ref.at[pl.ds(n * PIECES, PIECES)], got.at[n]),
                fetch(tally_ref.at[:, pl.ds(n * COLS, COLS)], tally.at[n]),
            )
        )
    late = [
        fetch(source, target)
        for source, target in (
            (weight_ref, weight), (pre_ref, pre_self), (cot_ref, cot), (x_t_ref, x_t)
        )
    ]
    for n in range(MEAN_STEPS):
        for copy in early[n]:
            copy.wait()
        rows = jnp.concatenate(
            [
                jnp.concatenate([got[n, 2 * e + half] for e in range(COLS // RQ)], axis=0)
                for half in range(2)
            ],
            axis=1,
        )
        part = jnp.dot(tally[n], rows, preferred_element_type=jnp.float32)
        if n == 0:
            acc[...] = part
        elif n < MEAN_STEPS - 1:
            acc[...] += part
        else:
            value = ((acc[...] + part) / K).astype(jnp.bfloat16)
            mean[...] = value
            mean_t[...] = value.T
    for copy in late:
        copy.wait()
    first = core_ref[0] == 0
    leaving = []
    for n in range(LATE):
        block = slice(n * HB, (n + 1) * HB)
        pre = pre_self[:, block] + jnp.dot(
            mean[...], weight[:, block], preferred_element_type=jnp.float32
        )
        square = pre * pre
        tangent = jnp.tanh(0.7978845608 * (pre + 0.044715 * pre * square))
        rest = 1.0 + tangent
        hidden[:, block] = (0.5 * pre * rest).astype(jnp.bfloat16)
        slope = 0.5 * rest + 0.5 * pre * (1.0 - tangent * tangent) * 0.7978845608 * (
            1.0 + 3.0 * 0.044715 * square
        )
        delta = (cot[:, block].astype(jnp.float32) * slope).astype(jnp.bfloat16)
        bias_term = jnp.sum(delta.astype(jnp.float32), axis=0, keepdims=True)
        grad_self = jnp.dot(x_t[...], delta, preferred_element_type=jnp.float32)
        grad_neigh = jnp.dot(mean_t[...], delta, preferred_element_type=jnp.float32)
        tail = jnp.broadcast_to(bias_term, (RBP - RB, HB))
        for ref, value in (
            (given, jnp.where(first, grad_neigh, grad_self)),
            (kept, jnp.where(first, grad_self, grad_neigh)),
        ):
            for c in range(HB // 128):
                lanes = slice(c * 128, (c + 1) * 128)
                for r in range(8):
                    ref[n, r, c] = jnp.concatenate(
                        [value[r * RB : (r + 1) * RB, lanes], tail[:, lanes]], axis=0
                    ).astype(jnp.bfloat16)
        chunk = pl.ds(n * (HB // 128), HB // 128)
        for e, (source, target) in enumerate(
            (
                (given.at[n], given_ref.at[:, chunk]),
                (kept.at[n], kept_ref.at[:, chunk]),
                (hidden.at[:, pl.ds(n * HB, HB)], hidden_ref.at[:, pl.ds(n * HB, HB)]),
            )
        ):
            copy = pltpu.make_async_copy(source, target, out_sem.at[3 * n + e])
            copy.start()
            leaving.append(copy)
    for copy in leaving:
        copy.wait()


def layer(core, got, tally, pre_self, x_t, weight_neigh, cotangent):
    whole = pl.BlockSpec(memory_space=pl.ANY)
    return pl.pallas_call(
        layer_kernel,
        in_specs=[pl.BlockSpec(memory_space=pltpu.SMEM)] + [whole] * 6,
        out_specs=[whole] * 3,
        out_shape=[
            jax.ShapeDtypeStruct((TGT, H), jnp.bfloat16),
            pltpu.VMEM((8, 8, RBP, 128), jnp.bfloat16),
            pltpu.VMEM((8, 8, RBP, 128), jnp.bfloat16),
        ],
        scratch_shapes=[
            pltpu.VMEM((MEAN_STEPS, PIECES, RQ, HALF), jnp.bfloat16),
            pltpu.VMEM((MEAN_STEPS, TGT, COLS), jnp.bfloat16),
            pltpu.VMEM((TGT, H), jnp.float32),
            pltpu.VMEM((F, TGT), jnp.bfloat16),
            pltpu.VMEM((F, H), jnp.bfloat16),
            pltpu.VMEM((TGT, H), jnp.bfloat16),
            pltpu.VMEM((TGT, H), jnp.bfloat16),
            pltpu.VMEM((LATE, 8, HB // 128, RBP, 128), jnp.bfloat16),
            pltpu.VMEM((LATE, 8, HB // 128, RBP, 128), jnp.bfloat16),
            pltpu.VMEM((TGT, F), jnp.float32),
            pltpu.VMEM((TGT, F), jnp.bfloat16),
            pltpu.VMEM((F, TGT), jnp.bfloat16),
            pltpu.SemaphoreType.DMA((2 * MEAN_STEPS + 4,)),
            pltpu.SemaphoreType.DMA((3 * LATE,)),
        ],
        compiler_params=pltpu.CompilerParams(vmem_limit_bytes=58 << 20),
        name="layer",
    )(core, got, tally, pre_self, x_t, weight_neigh, cotangent)


def unpack_kernel(core_ref, full_ref, theirs_ref, self_ref, neigh_ref, bias_ref):
    first = core_ref[0] == 0
    for r in range(2):
        rows = slice(r * RB, (r + 1) * RB)
        for c in range(8):
            lanes = slice(c * 128, (c + 1) * 128)
            a = full_ref[r, c].astype(jnp.float32)
            b = theirs_ref[r, c].astype(jnp.float32)
            self_ref[rows, lanes] = jnp.where(first, a[:RB], b[:RB])
            neigh_ref[rows, lanes] = jnp.where(first, b[:RB], a[:RB])
            bias_ref[:, lanes] = a[RB : RB + 1]


def unpack(core, full, theirs):
    chunks = pl.BlockSpec((2, 8, RBP, 128), lambda i, w: (i, 0, 0, 0))
    return pl.pallas_call(
        unpack_kernel,
        grid_spec=pltpu.PrefetchScalarGridSpec(
            num_scalar_prefetch=1,
            grid=(4,),
            in_specs=[chunks, chunks],
            out_specs=[
                pl.BlockSpec((2 * RB, H), lambda i, w: (i, 0)),
                pl.BlockSpec((2 * RB, H), lambda i, w: (i, 0)),
                pl.BlockSpec((1, H), lambda i, w: (0, 0)),
            ],
        ),
        out_shape=[
            jax.ShapeDtypeStruct((F, H), jnp.float32),
            jax.ShapeDtypeStruct((F, H), jnp.float32),
            jax.ShapeDtypeStruct((1, H), jnp.float32),
        ],
        compiler_params=pltpu.CompilerParams(vmem_limit_bytes=12 << 20),
        name="unpack",
    )(core, full.reshape(8, 8, RBP, 128), theirs.reshape(8, 8, RBP, 128))


def sum_over_devices(kept, given, core):
    kept = kept.reshape(CHIP_COUNT, RBP, 128)
    received = lax.ppermute(given.reshape(CHIP_COUNT, RBP, 128), "core", SWAP)
    chip = (kept.astype(jnp.float32) + received.astype(jnp.float32)).astype(jnp.bfloat16)
    parts = exchange(chip, CHIPS)
    mine = jnp.sum(parts.astype(jnp.float32), axis=0).astype(jnp.bfloat16)
    full = exchange(jnp.broadcast_to(mine[None], (CHIP_COUNT, RBP, 128)), CHIPS)
    theirs = lax.ppermute(full, "core", SWAP)
    grad_self, grad_neigh, grad_bias = unpack(core, full, theirs)
    return grad_self, grad_neigh, grad_bias.reshape(H)


def local(
    node_codes, node_scales, target_rows, owners, local_blocks, neighbours,
    weight_self, weight_neigh, bias, cotangent,
):
    core = lax.axis_index("core")
    owner = owners[:, 0]
    owner_core = (owner // 16) % 2
    owner_chip = (owner // 32) * 16 + owner % 16
    serving = (jnp.arange(R_DEV, dtype=jnp.int32) // RQ) % 2
    place = (owner_core != serving).astype(jnp.int32) * TABLE + owner_chip * NB_DEV + local_blocks
    place = place * SLOT
    asked = jnp.broadcast_to(place.reshape(1, 2, 1, RQ), (4, 2, 16, RQ)).reshape(DEVICES, RQ)
    wanted = exchange(asked, ALL)

    stripes = make_stripes(node_codes, node_scales.astype(jnp.float32))
    own = exchange(stripes.reshape(CHIP_COUNT, NB_DEV, HALF), CHIPS)
    own = own.reshape(TABLE, HALF)
    sister = lax.ppermute(own, "core", SWAP)
    send = gather(wanted, own, sister)
    send, neighbours, target_rows = lax.optimization_barrier((send, neighbours, target_rows))
    got = exchange(send, ALL)

    block, row = neighbours // BR, neighbours % BR
    column = (row // 8) * 1024 + (block // RQ) * 512 + (row % 8) * RQ + block % RQ
    x_t, pre_self, tally = side(
        target_rows, column, node_codes, node_scales.astype(jnp.float32), weight_self, bias
    )
    which = core.reshape(1).astype(jnp.int32)
    hidden, kept, given = layer(
        which, got, tally, pre_self, x_t, weight_neigh, cotangent
    )
    return (hidden,) + sum_over_devices(kept, given, which)


def solution(mesh):
    fine = Mesh(mesh.devices.reshape(4, 2, 4, 4), ALL)
    placed = (
        P(ALL, None),
        P(ALL),
        P(ALL),
        P(ALL, None),
        P(ALL),
        P(ALL, None),
        P(),
        P(),
        P(),
        P(ALL, None),
    )
    return jax.shard_map(
        local,
        mesh=fine,
        in_specs=placed,
        out_specs=(P(ALL, None), P(), P(), P()),
        check_vma=False,
    )
```

```python
import jax
import jax.numpy as jnp
from jax import lax
from jax.experimental import pallas as pl
from jax.experimental.pallas import tpu as pltpu
from jax.sharding import Mesh, PartitionSpec as P

F = 768
H = 1024
BR = 32
K = 10
NODE_DEV = 2048
TGT = 1024
NB_DEV = 64
R_DEV = 128
CHIP_COUNT = 64
DEVICES = 128
HALF = F // 2
RQ = R_DEV // 2
ALL = ("z", "core", "x", "y")
CHIPS = ("z", "x", "y")
SWAP = [(0, 1), (1, 0)]
HB = 256
RB = 96
RBP = 104


def exchange(array, axes):
    return lax.all_to_all(array, axes, split_axis=0, concat_axis=0, tiled=True)


PITCH = BR + 4


def stripe_copy(codes_ref, codes, sem, k):
    lanes = pl.ds(pl.multiple_of(k * 128, 128), 128)
    return pltpu.make_async_copy(codes_ref.at[:, lanes], codes.at[k], sem.at[k])


def stripe_kernel(codes_ref, scales_ref, stripes_ref, codes, scales, wide, sem):
    k = pl.program_id(0)

    @pl.when(k == 0)
    def _():
        for n in range(6):
            stripe_copy(codes_ref, codes, sem, n).start()
        columns = scales_ref[...].T
        for c in range(NODE_DEV // 128):
            scales[c * 128 : (c + 1) * 128, :] = jnp.broadcast_to(columns[:, c : c + 1], (128, 128))

    stripe_copy(codes_ref, codes, sem, k).wait()
    product = codes[k].astype(jnp.float32) * scales[...]
    for b in range(NB_DEV):
        wide[b * PITCH : b * PITCH + BR, :] = product[b * BR : (b + 1) * BR]
    for row in range(BR):
        stripes_ref[row, 0] = wide[pl.ds(row, NB_DEV, stride=PITCH), :].astype(jnp.bfloat16)


def make_stripes(codes, scales):
    return pl.pallas_call(
        stripe_kernel,
        grid=(6,),
        in_specs=[
            pl.BlockSpec(memory_space=pl.ANY),
            pl.BlockSpec((NODE_DEV // 128, 128), lambda k: (0, 0)),
        ],
        out_specs=pl.BlockSpec((BR, 1, NB_DEV, 128), lambda k: (0, k // 3, 0, k % 3)),
        out_shape=jax.ShapeDtypeStruct((BR, 2, NB_DEV, HALF), jnp.bfloat16),
        scratch_shapes=[
            pltpu.VMEM((6, NODE_DEV, 128), jnp.bfloat16),
            pltpu.VMEM((NODE_DEV, 128), jnp.float32),
            pltpu.VMEM((NB_DEV * PITCH, 128), jnp.float32),
            pltpu.SemaphoreType.DMA((6,)),
        ],
        compiler_params=pltpu.CompilerParams(vmem_limit_bytes=60 << 20),
        name="make_stripes",
    )(codes, scales.reshape(NODE_DEV // 128, 128))


GROUP = 16
TABLE = CHIP_COUNT * NB_DEV
SLOT = 4


STAGES = 8
STAGE = 2 * TABLE // STAGES


def gather_kernel(wanted_ref, own_ref, sister_ref, out_ref, table, picked, narrow, sem):
    @pl.when(pl.program_id(0) == 0)
    def _():
        copies = []
        for n in range(STAGES):
            source = own_ref if n < STAGES // 2 else sister_ref
            start = n % (STAGES // 2) * STAGE
            copies.append(
                pltpu.make_async_copy(source.at[pl.ds(start, STAGE)], narrow.at[n], sem.at[n])
            )
            copies[-1].start()
        for n in range(STAGES):
            copies[n].wait()
            for k in range(3):
                table[pl.ds(n * STAGE * SLOT + k, STAGE, stride=SLOT), :] = narrow[
                    n, :, k * 128 : (k + 1) * 128
                ].astype(jnp.float32)

    first = pl.program_id(0) * GROUP

    def pair(step, carry):
        for u in range(2):
            base = u * RQ * SLOT
            for j in range(RQ):
                at = pl.multiple_of(wanted_ref[first + 2 * step + u, j], SLOT)
                picked[pl.ds(base + j * SLOT, SLOT), :] = table[pl.ds(at, SLOT), :]
            for k in range(3):
                out_ref[2 * step + u, :, k * 128 : (k + 1) * 128] = picked[
                    pl.ds(base + k, RQ, stride=SLOT), :
                ].astype(jnp.bfloat16)
        return carry

    lax.fori_loop(0, GROUP // 2, pair, 0)


def gather(wanted, own, sister):
    return pl.pallas_call(
        gather_kernel,
        grid_spec=pltpu.PrefetchScalarGridSpec(
            num_scalar_prefetch=1,
            grid=(DEVICES // GROUP,),
            in_specs=[
                pl.BlockSpec(memory_space=pl.ANY),
                pl.BlockSpec(memory_space=pl.ANY),
            ],
            out_specs=pl.BlockSpec((GROUP, RQ, HALF), lambda i, w: (i, 0, 0)),
            scratch_shapes=[
                pltpu.VMEM((2 * TABLE * SLOT, 128), jnp.float32),
                pltpu.VMEM((2 * RQ * SLOT, 128), jnp.float32),
                pltpu.VMEM((STAGES, STAGE, HALF), jnp.bfloat16),
                pltpu.SemaphoreType.DMA((STAGES,)),
            ],
        ),
        out_shape=pltpu.HBM((DEVICES, RQ, HALF), jnp.bfloat16),
        compiler_params=pltpu.CompilerParams(vmem_limit_bytes=27 << 20),
        name="gather_rows",
    )(wanted, own, sister)


SIDE = 128


def side_kernel(
    target_ref, column_ref, codes_ref, scales_ref, weight_ref, bias_ref, x_t_ref, pre_ref, tally_ref
):
    hit = target_ref[...] == lax.broadcasted_iota(jnp.int32, (SIDE, NODE_DEV), 1)
    picker = hit.astype(jnp.float32).astype(jnp.bfloat16)
    own_codes = jnp.dot(picker, codes_ref[...], preferred_element_type=jnp.float32)
    own_scales = jnp.sum(jnp.where(hit, scales_ref[...], 0.0), axis=1, keepdims=True)
    x_self = (own_codes * own_scales).astype(jnp.bfloat16)
    x_t_ref[...] = x_self.T
    pre_ref[...] = bias_ref[...] + jnp.dot(
        x_self, weight_ref[...], preferred_element_type=jnp.float32
    )
    wide = 256

    def count(c, carry):
        first = pl.multiple_of(c * wide, wide)
        ids = lax.broadcasted_iota(jnp.int32, (SIDE, wide), 1) + first
        total = jnp.zeros((SIDE, wide), jnp.float32)
        for k in range(K):
            total = total + jnp.where(column_ref[:, k : k + 1] == ids, 1.0, 0.0)
        tally_ref[:, pl.ds(first, wide)] = total.astype(jnp.bfloat16)
        return carry

    lax.fori_loop(0, R_DEV * BR // wide, count, 0)


def side(targets, columns, codes, scales, weight, bias):
    same = lambda i: (0, 0)
    return pl.pallas_call(
        side_kernel,
        grid=(TGT // SIDE,),
        in_specs=[
            pl.BlockSpec((SIDE, 1), lambda i: (i, 0)),
            pl.BlockSpec((SIDE, K), lambda i: (i, 0)),
            pl.BlockSpec((NODE_DEV, F), same),
            pl.BlockSpec((1, NODE_DEV), same),
            pl.BlockSpec((F, H), same),
            pl.BlockSpec((1, H), same),
        ],
        out_specs=[
            pl.BlockSpec((F, SIDE), lambda i: (0, i)),
            pl.BlockSpec((SIDE, H), lambda i: (i, 0)),
            pl.BlockSpec((SIDE, R_DEV * BR), lambda i: (i, 0)),
        ],
        out_shape=[
            jax.ShapeDtypeStruct((F, TGT), jnp.bfloat16),
            jax.ShapeDtypeStruct((TGT, H), jnp.float32),
            jax.ShapeDtypeStruct((TGT, R_DEV * BR), jnp.bfloat16),
        ],
        compiler_params=pltpu.CompilerParams(vmem_limit_bytes=24 << 20),
        name="side",
    )(targets[:, None], columns, codes, scales[None, :], weight, bias[None, :])


MEAN_STEPS = 4
COLS = R_DEV * BR // MEAN_STEPS
PIECES = DEVICES // MEAN_STEPS
LATE = H // HB


def layer_kernel(
    core_ref, got_ref, tally_ref, pre_ref, x_t_ref, weight_ref, cot_ref,
    hidden_ref, kept_ref, given_ref,
    got, tally, pre_self, x_t, weight, cot, hidden, acc, mean, mean_t, sem, out_sem,
):
    count = 0

    def fetch(source, target):
        nonlocal count
        copy = pltpu.make_async_copy(source, target, sem.at[count])
        count += 1
        copy.start()
        return copy

    early = []
    for n in range(MEAN_STEPS):
        early.append(
            (
                fetch(got_ref.at[pl.ds(n * PIECES, PIECES)], got.at[n]),
                fetch(tally_ref.at[:, pl.ds(n * COLS, COLS)], tally.at[n]),
            )
        )
    late = [
        fetch(source, target)
        for source, target in (
            (weight_ref, weight), (pre_ref, pre_self), (cot_ref, cot), (x_t_ref, x_t)
        )
    ]
    for n in range(MEAN_STEPS):
        for copy in early[n]:
            copy.wait()
        rows = jnp.concatenate(
            [
                jnp.concatenate([got[n, 2 * e + half] for e in range(COLS // RQ)], axis=0)
                for half in range(2)
            ],
            axis=1,
        )
        part = jnp.dot(tally[n], rows, preferred_element_type=jnp.float32)
        if n == 0:
            acc[...] = part
        elif n < MEAN_STEPS - 1:
            acc[...] += part
        else:
            value = ((acc[...] + part) / K).astype(jnp.bfloat16)
            mean[...] = value
            mean_t[...] = value.T
    for copy in late:
        copy.wait()
    first = core_ref[0] == 0
    leaving = []
    for n in range(LATE):
        block = slice(n * HB, (n + 1) * HB)
        pre = pre_self[:, block] + jnp.dot(
            mean[...], weight[:, block], preferred_element_type=jnp.float32
        )
        square = pre * pre
        tangent = jnp.tanh(0.7978845608 * (pre + 0.044715 * pre * square))
        rest = 1.0 + tangent
        hidden[:, block] = (0.5 * pre * rest).astype(jnp.bfloat16)
        slope = 0.5 * rest + 0.5 * pre * (1.0 - tangent * tangent) * 0.7978845608 * (
            1.0 + 3.0 * 0.044715 * square
        )
        delta = (cot[:, block].astype(jnp.float32) * slope).astype(jnp.bfloat16)
        bias_term = jnp.sum(delta.astype(jnp.float32), axis=0, keepdims=True)
        grad_self = jnp.dot(x_t[...], delta, preferred_element_type=jnp.float32)
        grad_neigh = jnp.dot(mean_t[...], delta, preferred_element_type=jnp.float32)
        tail = jnp.broadcast_to(bias_term, (RBP - RB, HB))
        for ref, value in (
            (given_ref, jnp.where(first, grad_neigh, grad_self)),
            (kept_ref, jnp.where(first, grad_self, grad_neigh)),
        ):
            for c in range(HB // 128):
                lanes = slice(c * 128, (c + 1) * 128)
                for r in range(8):
                    ref[r, n * (HB // 128) + c] = jnp.concatenate(
                        [value[r * RB : (r + 1) * RB, lanes], tail[:, lanes]], axis=0
                    ).astype(jnp.bfloat16)
        lanes = pl.ds(n * HB, HB)
        copy = pltpu.make_async_copy(hidden.at[:, lanes], hidden_ref.at[:, lanes], out_sem.at[n])
        copy.start()
        leaving.append(copy)
    for copy in leaving:
        copy.wait()


def layer(core, got, tally, pre_self, x_t, weight_neigh, cotangent):
    whole = pl.BlockSpec(memory_space=pl.ANY)
    return pl.pallas_call(
        layer_kernel,
        in_specs=[pl.BlockSpec(memory_space=pltpu.SMEM)] + [whole] * 6,
        out_specs=[whole] + [pl.BlockSpec(memory_space=pltpu.VMEM)] * 2,
        out_shape=[
            jax.ShapeDtypeStruct((TGT, H), jnp.bfloat16),
            pltpu.VMEM((8, 8, RBP, 128), jnp.bfloat16),
            pltpu.VMEM((8, 8, RBP, 128), jnp.bfloat16),
        ],
        scratch_shapes=[
            pltpu.VMEM((MEAN_STEPS, PIECES, RQ, HALF), jnp.bfloat16),
            pltpu.VMEM((MEAN_STEPS, TGT, COLS), jnp.bfloat16),
            pltpu.VMEM((TGT, H), jnp.float32),
            pltpu.VMEM((F, TGT), jnp.bfloat16),
            pltpu.VMEM((F, H), jnp.bfloat16),
            pltpu.VMEM((TGT, H), jnp.bfloat16),
            pltpu.VMEM((TGT, H), jnp.bfloat16),
            pltpu.VMEM((TGT, F), jnp.float32),
            pltpu.VMEM((TGT, F), jnp.bfloat16),
            pltpu.VMEM((F, TGT), jnp.bfloat16),
            pltpu.SemaphoreType.DMA((2 * MEAN_STEPS + 4,)),
            pltpu.SemaphoreType.DMA((LATE,)),
        ],
        compiler_params=pltpu.CompilerParams(vmem_limit_bytes=58 << 20),
        name="layer",
    )(core, got, tally, pre_self, x_t, weight_neigh, cotangent)


def unpack_kernel(core_ref, full_ref, theirs_ref, self_ref, neigh_ref, bias_ref):
    first = core_ref[0] == 0
    for r in range(2):
        rows = slice(r * RB, (r + 1) * RB)
        for c in range(8):
            lanes = slice(c * 128, (c + 1) * 128)
            a = full_ref[r, c].astype(jnp.float32)
            b = theirs_ref[r, c].astype(jnp.float32)
            self_ref[rows, lanes] = jnp.where(first, a[:RB], b[:RB])
            neigh_ref[rows, lanes] = jnp.where(first, b[:RB], a[:RB])
            bias_ref[:, lanes] = a[RB : RB + 1]


def unpack(core, full, theirs):
    chunks = pl.BlockSpec((2, 8, RBP, 128), lambda i, w: (i, 0, 0, 0))
    return pl.pallas_call(
        unpack_kernel,
        grid_spec=pltpu.PrefetchScalarGridSpec(
            num_scalar_prefetch=1,
            grid=(4,),
            in_specs=[chunks, chunks],
            out_specs=[
                pl.BlockSpec((2 * RB, H), lambda i, w: (i, 0)),
                pl.BlockSpec((2 * RB, H), lambda i, w: (i, 0)),
                pl.BlockSpec((1, H), lambda i, w: (0, 0)),
            ],
        ),
        out_shape=[
            jax.ShapeDtypeStruct((F, H), jnp.float32),
            jax.ShapeDtypeStruct((F, H), jnp.float32),
            jax.ShapeDtypeStruct((1, H), jnp.float32),
        ],
        compiler_params=pltpu.CompilerParams(vmem_limit_bytes=12 << 20),
        name="unpack",
    )(core, full.reshape(8, 8, RBP, 128), theirs.reshape(8, 8, RBP, 128))


def sum_over_devices(kept, given, core):
    kept = kept.reshape(CHIP_COUNT, RBP, 128)
    received = lax.ppermute(given.reshape(CHIP_COUNT, RBP, 128), "core", SWAP)
    chip = (kept.astype(jnp.float32) + received.astype(jnp.float32)).astype(jnp.bfloat16)
    parts = exchange(chip, CHIPS)
    mine = jnp.sum(parts.astype(jnp.float32), axis=0).astype(jnp.bfloat16)
    full = exchange(jnp.broadcast_to(mine[None], (CHIP_COUNT, RBP, 128)), CHIPS)
    theirs = lax.ppermute(full, "core", SWAP)
    grad_self, grad_neigh, grad_bias = unpack(core, full, theirs)
    return grad_self, grad_neigh, grad_bias.reshape(H)


def local(
    node_codes, node_scales, target_rows, owners, local_blocks, neighbours,
    weight_self, weight_neigh, bias, cotangent,
):
    core = lax.axis_index("core")
    owner = owners[:, 0]
    owner_core = (owner // 16) % 2
    owner_chip = (owner // 32) * 16 + owner % 16
    serving = (jnp.arange(R_DEV, dtype=jnp.int32) // RQ) % 2
    place = (owner_core != serving).astype(jnp.int32) * TABLE + owner_chip * NB_DEV + local_blocks
    place = place * SLOT
    asked = jnp.broadcast_to(place.reshape(1, 2, 1, RQ), (4, 2, 16, RQ)).reshape(DEVICES, RQ)
    wanted = exchange(asked, ALL)

    stripes = make_stripes(node_codes, node_scales.astype(jnp.float32))
    own = exchange(stripes.reshape(CHIP_COUNT, NB_DEV, HALF), CHIPS)
    own = own.reshape(TABLE, HALF)
    sister = lax.ppermute(own, "core", SWAP)
    send = gather(wanted, own, sister)
    send, neighbours, target_rows = lax.optimization_barrier((send, neighbours, target_rows))
    got = exchange(send, ALL)

    block, row = neighbours // BR, neighbours % BR
    column = (row // 8) * 1024 + (block // RQ) * 512 + (row % 8) * RQ + block % RQ
    x_t, pre_self, tally = side(
        target_rows, column, node_codes, node_scales.astype(jnp.float32), weight_self, bias
    )
    which = core.reshape(1).astype(jnp.int32)
    hidden, kept, given = layer(
        which, got, tally, pre_self, x_t, weight_neigh, cotangent
    )
    return (hidden,) + sum_over_devices(kept, given, which)


def solution(mesh):
    fine = Mesh(mesh.devices.reshape(4, 2, 4, 4), ALL)
    placed = (
        P(ALL, None),
        P(ALL),
        P(ALL),
        P(ALL, None),
        P(ALL),
        P(ALL, None),
        P(),
        P(),
        P(),
        P(ALL, None),
    )
    return jax.shard_map(
        local,
        mesh=fine,
        in_specs=placed,
        out_specs=(P(ALL, None), P(), P(), P()),
        check_vma=False,
    )
```

```python
import jax
import jax.numpy as jnp
from jax import lax
from jax.experimental import pallas as pl
from jax.experimental.pallas import tpu as pltpu
from jax.sharding import Mesh, PartitionSpec as P

F = 768
H = 1024
BR = 32
K = 10
NODE_DEV = 2048
TGT = 1024
NB_DEV = 64
R_DEV = 128
CHIP_COUNT = 64
DEVICES = 128
HALF = F // 2
RQ = R_DEV // 2
ALL = ("z", "core", "x", "y")
CHIPS = ("z", "x", "y")
SWAP = [(0, 1), (1, 0)]
HB = 256
RB = 96
RBP = 104


def exchange(array, axes):
    return lax.all_to_all(array, axes, split_axis=0, concat_axis=0, tiled=True)


PITCH = BR + 4


def stripe_copy(codes_ref, codes, sem, k):
    lanes = pl.ds(pl.multiple_of(k * 128, 128), 128)
    return pltpu.make_async_copy(codes_ref.at[:, lanes], codes.at[k], sem.at[k])


def stripe_kernel(codes_ref, scales_ref, stripes_ref, codes, scales, wide, sem):
    k = pl.program_id(0)

    @pl.when(k == 0)
    def _():
        for n in range(6):
            stripe_copy(codes_ref, codes, sem, n).start()
        columns = scales_ref[...].T
        for c in range(NODE_DEV // 128):
            scales[c * 128 : (c + 1) * 128, :] = jnp.broadcast_to(columns[:, c : c + 1], (128, 128))

    stripe_copy(codes_ref, codes, sem, k).wait()
    product = codes[k].astype(jnp.float32) * scales[...]
    for b in range(NB_DEV):
        wide[b * PITCH : b * PITCH + BR, :] = product[b * BR : (b + 1) * BR]
    for row in range(BR):
        stripes_ref[row, 0] = wide[pl.ds(row, NB_DEV, stride=PITCH), :].astype(jnp.bfloat16)


def make_stripes(codes, scales):
    return pl.pallas_call(
        stripe_kernel,
        grid=(6,),
        in_specs=[
            pl.BlockSpec(memory_space=pl.ANY),
            pl.BlockSpec((NODE_DEV // 128, 128), lambda k: (0, 0)),
        ],
        out_specs=pl.BlockSpec((BR, 1, NB_DEV, 128), lambda k: (0, k // 3, 0, k % 3)),
        out_shape=jax.ShapeDtypeStruct((BR, 2, NB_DEV, HALF), jnp.bfloat16),
        scratch_shapes=[
            pltpu.VMEM((6, NODE_DEV, 128), jnp.bfloat16),
            pltpu.VMEM((NODE_DEV, 128), jnp.float32),
            pltpu.VMEM((NB_DEV * PITCH, 128), jnp.float32),
            pltpu.SemaphoreType.DMA((6,)),
        ],
        compiler_params=pltpu.CompilerParams(vmem_limit_bytes=60 << 20),
        name="make_stripes",
    )(codes, scales.reshape(NODE_DEV // 128, 128))


GROUP = 16
TABLE = CHIP_COUNT * NB_DEV
SLOT = 4


STAGES = 8
STAGE = 2 * TABLE // STAGES


def gather_kernel(wanted_ref, own_ref, sister_ref, out_ref, table, picked, narrow, sem):
    @pl.when(pl.program_id(0) == 0)
    def _():
        copies = []
        for n in range(STAGES):
            source = own_ref if n < STAGES // 2 else sister_ref
            start = n % (STAGES // 2) * STAGE
            copies.append(
                pltpu.make_async_copy(source.at[pl.ds(start, STAGE)], narrow.at[n], sem.at[n])
            )
            copies[-1].start()
        for n in range(STAGES):
            copies[n].wait()
            for k in range(3):
                table[pl.ds(n * STAGE * SLOT + k, STAGE, stride=SLOT), :] = narrow[
                    n, :, k * 128 : (k + 1) * 128
                ].astype(jnp.float32)

    first = pl.program_id(0) * GROUP

    def pair(step, carry):
        for u in range(2):
            base = u * RQ * SLOT
            for j in range(RQ):
                at = pl.multiple_of(wanted_ref[first + 2 * step + u, j], SLOT)
                picked[pl.ds(base + j * SLOT, SLOT), :] = table[pl.ds(at, SLOT), :]
        for u in range(2):
            base = u * RQ * SLOT
            for k in range(3):
                out_ref[2 * step + u, :, k * 128 : (k + 1) * 128] = picked[
                    pl.ds(base + k, RQ, stride=SLOT), :
                ].astype(jnp.bfloat16)
        return carry

    lax.fori_loop(0, GROUP // 2, pair, 0)


def gather(wanted, own, sister):
    return pl.pallas_call(
        gather_kernel,
        grid_spec=pltpu.PrefetchScalarGridSpec(
            num_scalar_prefetch=1,
            grid=(DEVICES // GROUP,),
            in_specs=[
                pl.BlockSpec(memory_space=pl.ANY),
                pl.BlockSpec(memory_space=pl.ANY),
            ],
            out_specs=pl.BlockSpec((GROUP, RQ, HALF), lambda i, w: (i, 0, 0)),
            scratch_shapes=[
                pltpu.VMEM((2 * TABLE * SLOT, 128), jnp.float32),
                pltpu.VMEM((2 * RQ * SLOT, 128), jnp.float32),
                pltpu.VMEM((STAGES, STAGE, HALF), jnp.bfloat16),
                pltpu.SemaphoreType.DMA((STAGES,)),
            ],
        ),
        out_shape=pltpu.HBM((DEVICES, RQ, HALF), jnp.bfloat16),
        compiler_params=pltpu.CompilerParams(vmem_limit_bytes=27 << 20),
        name="gather_rows",
    )(wanted, own, sister)


SIDE = 128


def side_kernel(
    target_ref, column_ref, codes_ref, scales_ref, weight_ref, bias_ref, x_t_ref, pre_ref, tally_ref
):
    hit = target_ref[...] == lax.broadcasted_iota(jnp.int32, (SIDE, NODE_DEV), 1)
    picker = hit.astype(jnp.float32).astype(jnp.bfloat16)
    own_codes = jnp.dot(picker, codes_ref[...], preferred_element_type=jnp.float32)
    own_scales = jnp.sum(jnp.where(hit, scales_ref[...], 0.0), axis=1, keepdims=True)
    x_self = (own_codes * own_scales).astype(jnp.bfloat16)
    x_t_ref[...] = x_self.T
    pre_ref[...] = bias_ref[...] + jnp.dot(
        x_self, weight_ref[...], preferred_element_type=jnp.float32
    )
    wide = 256

    def count(c, carry):
        first = pl.multiple_of(c * wide, wide)
        ids = lax.broadcasted_iota(jnp.int32, (SIDE, wide), 1) + first
        total = jnp.zeros((SIDE, wide), jnp.float32)
        for k in range(K):
            total = total + jnp.where(column_ref[:, k : k + 1] == ids, 1.0, 0.0)
        tally_ref[:, pl.ds(first, wide)] = total.astype(jnp.bfloat16)
        return carry

    lax.fori_loop(0, R_DEV * BR // wide, count, 0)


def side(targets, columns, codes, scales, weight, bias):
    same = lambda i: (0, 0)
    return pl.pallas_call(
        side_kernel,
        grid=(TGT // SIDE,),
        in_specs=[
            pl.BlockSpec((SIDE, 1), lambda i: (i, 0)),
            pl.BlockSpec((SIDE, K), lambda i: (i, 0)),
            pl.BlockSpec((NODE_DEV, F), same),
            pl.BlockSpec((1, NODE_DEV), same),
            pl.BlockSpec((F, H), same),
            pl.BlockSpec((1, H), same),
        ],
        out_specs=[
            pl.BlockSpec((F, SIDE), lambda i: (0, i)),
            pl.BlockSpec((SIDE, H), lambda i: (i, 0)),
            pl.BlockSpec((SIDE, R_DEV * BR), lambda i: (i, 0)),
        ],
        out_shape=[
            jax.ShapeDtypeStruct((F, TGT), jnp.bfloat16),
            jax.ShapeDtypeStruct((TGT, H), jnp.float32),
            jax.ShapeDtypeStruct((TGT, R_DEV * BR), jnp.bfloat16),
        ],
        compiler_params=pltpu.CompilerParams(vmem_limit_bytes=24 << 20),
        name="side",
    )(targets[:, None], columns, codes, scales[None, :], weight, bias[None, :])


MEAN_STEPS = 4
COLS = R_DEV * BR // MEAN_STEPS
PIECES = DEVICES // MEAN_STEPS
LATE = H // HB


def layer_kernel(
    core_ref, got_ref, tally_ref, pre_ref, x_t_ref, weight_ref, cot_ref,
    hidden_ref, kept_ref, given_ref,
    got, tally, pre_self, x_t, weight, cot, hidden, acc, mean, mean_t, sem, out_sem,
):
    count = 0

    def fetch(source, target):
        nonlocal count
        copy = pltpu.make_async_copy(source, target, sem.at[count])
        count += 1
        copy.start()
        return copy

    early = []
    for n in range(MEAN_STEPS):
        early.append(
            (
                fetch(got_ref.at[pl.ds(n * PIECES, PIECES)], got.at[n]),
                fetch(tally_ref.at[:, pl.ds(n * COLS, COLS)], tally.at[n]),
            )
        )
    late = [
        fetch(source, target)
        for source, target in (
            (weight_ref, weight), (pre_ref, pre_self), (cot_ref, cot), (x_t_ref, x_t)
        )
    ]
    for n in range(MEAN_STEPS):
        for copy in early[n]:
            copy.wait()
        rows = jnp.concatenate(
            [
                jnp.concatenate([got[n, 2 * e + half] for e in range(COLS // RQ)], axis=0)
                for half in range(2)
            ],
            axis=1,
        )
        part = jnp.dot(tally[n], rows, preferred_element_type=jnp.float32)
        if n == 0:
            acc[...] = part
        elif n < MEAN_STEPS - 1:
            acc[...] += part
        else:
            value = ((acc[...] + part) / K).astype(jnp.bfloat16)
            mean[...] = value
            mean_t[...] = value.T
    for copy in late:
        copy.wait()
    first = core_ref[0] == 0
    leaving = []
    for n in range(LATE):
        block = slice(n * HB, (n + 1) * HB)
        pre = pre_self[:, block] + jnp.dot(
            mean[...], weight[:, block], preferred_element_type=jnp.float32
        )
        square = pre * pre
        tangent = jnp.tanh(0.7978845608 * (pre + 0.044715 * pre * square))
        rest = 1.0 + tangent
        hidden[:, block] = (0.5 * pre * rest).astype(jnp.bfloat16)
        slope = 0.5 * rest + 0.5 * pre * (1.0 - tangent * tangent) * 0.7978845608 * (
            1.0 + 3.0 * 0.044715 * square
        )
        delta = (cot[:, block].astype(jnp.float32) * slope).astype(jnp.bfloat16)
        bias_term = jnp.sum(delta.astype(jnp.float32), axis=0, keepdims=True)
        grad_self = jnp.dot(x_t[...], delta, preferred_element_type=jnp.float32)
        grad_neigh = jnp.dot(mean_t[...], delta, preferred_element_type=jnp.float32)
        tail = jnp.broadcast_to(bias_term, (RBP - RB, HB))
        for ref, value in (
            (given_ref, jnp.where(first, grad_neigh, grad_self)),
            (kept_ref, jnp.where(first, grad_self, grad_neigh)),
        ):
            for c in range(HB // 128):
                lanes = slice(c * 128, (c + 1) * 128)
                for r in range(8):
                    ref[r, n * (HB // 128) + c] = jnp.concatenate(
                        [value[r * RB : (r + 1) * RB, lanes], tail[:, lanes]], axis=0
                    ).astype(jnp.bfloat16)
        lanes = pl.ds(n * HB, HB)
        copy = pltpu.make_async_copy(hidden.at[:, lanes], hidden_ref.at[:, lanes], out_sem.at[n])
        copy.start()
        leaving.append(copy)
    for copy in leaving:
        copy.wait()


def layer(core, got, tally, pre_self, x_t, weight_neigh, cotangent):
    whole = pl.BlockSpec(memory_space=pl.ANY)
    return pl.pallas_call(
        layer_kernel,
        in_specs=[pl.BlockSpec(memory_space=pltpu.SMEM)] + [whole] * 6,
        out_specs=[whole] + [pl.BlockSpec(memory_space=pltpu.VMEM)] * 2,
        out_shape=[
            jax.ShapeDtypeStruct((TGT, H), jnp.bfloat16),
            pltpu.VMEM((8, 8, RBP, 128), jnp.bfloat16),
            pltpu.VMEM((8, 8, RBP, 128), jnp.bfloat16),
        ],
        scratch_shapes=[
            pltpu.VMEM((MEAN_STEPS, PIECES, RQ, HALF), jnp.bfloat16),
            pltpu.VMEM((MEAN_STEPS, TGT, COLS), jnp.bfloat16),
            pltpu.VMEM((TGT, H), jnp.float32),
            pltpu.VMEM((F, TGT), jnp.bfloat16),
            pltpu.VMEM((F, H), jnp.bfloat16),
            pltpu.VMEM((TGT, H), jnp.bfloat16),
            pltpu.VMEM((TGT, H), jnp.bfloat16),
            pltpu.VMEM((TGT, F), jnp.float32),
            pltpu.VMEM((TGT, F), jnp.bfloat16),
            pltpu.VMEM((F, TGT), jnp.bfloat16),
            pltpu.SemaphoreType.DMA((2 * MEAN_STEPS + 4,)),
            pltpu.SemaphoreType.DMA((LATE,)),
        ],
        compiler_params=pltpu.CompilerParams(vmem_limit_bytes=58 << 20),
        name="layer",
    )(core, got, tally, pre_self, x_t, weight_neigh, cotangent)


def unpack_kernel(core_ref, full_ref, theirs_ref, self_ref, neigh_ref, bias_ref):
    first = core_ref[0] == 0
    for r in range(2):
        rows = slice(r * RB, (r + 1) * RB)
        for c in range(8):
            lanes = slice(c * 128, (c + 1) * 128)
            a = full_ref[r, c].astype(jnp.float32)
            b = theirs_ref[r, c].astype(jnp.float32)
            self_ref[rows, lanes] = jnp.where(first, a[:RB], b[:RB])
            neigh_ref[rows, lanes] = jnp.where(first, b[:RB], a[:RB])
            bias_ref[:, lanes] = a[RB : RB + 1]


def unpack(core, full, theirs):
    chunks = pl.BlockSpec((2, 8, RBP, 128), lambda i, w: (i, 0, 0, 0))
    return pl.pallas_call(
        unpack_kernel,
        grid_spec=pltpu.PrefetchScalarGridSpec(
            num_scalar_prefetch=1,
            grid=(4,),
            in_specs=[chunks, chunks],
            out_specs=[
                pl.BlockSpec((2 * RB, H), lambda i, w: (i, 0)),
                pl.BlockSpec((2 * RB, H), lambda i, w: (i, 0)),
                pl.BlockSpec((1, H), lambda i, w: (0, 0)),
            ],
        ),
        out_shape=[
            jax.ShapeDtypeStruct((F, H), jnp.float32),
            jax.ShapeDtypeStruct((F, H), jnp.float32),
            jax.ShapeDtypeStruct((1, H), jnp.float32),
        ],
        compiler_params=pltpu.CompilerParams(vmem_limit_bytes=12 << 20),
        name="unpack",
    )(core, full.reshape(8, 8, RBP, 128), theirs.reshape(8, 8, RBP, 128))


def sum_over_devices(kept, given, core):
    kept = kept.reshape(CHIP_COUNT, RBP, 128)
    received = lax.ppermute(given.reshape(CHIP_COUNT, RBP, 128), "core", SWAP)
    chip = (kept.astype(jnp.float32) + received.astype(jnp.float32)).astype(jnp.bfloat16)
    parts = exchange(chip, CHIPS)
    mine = jnp.sum(parts.astype(jnp.float32), axis=0).astype(jnp.bfloat16)
    full = exchange(jnp.broadcast_to(mine[None], (CHIP_COUNT, RBP, 128)), CHIPS)
    theirs = lax.ppermute(full, "core", SWAP)
    grad_self, grad_neigh, grad_bias = unpack(core, full, theirs)
    return grad_self, grad_neigh, grad_bias.reshape(H)


def local(
    node_codes, node_scales, target_rows, owners, local_blocks, neighbours,
    weight_self, weight_neigh, bias, cotangent,
):
    core = lax.axis_index("core")
    owner = owners[:, 0]
    owner_core = (owner // 16) % 2
    owner_chip = (owner // 32) * 16 + owner % 16
    serving = (jnp.arange(R_DEV, dtype=jnp.int32) // RQ) % 2
    place = (owner_core != serving).astype(jnp.int32) * TABLE + owner_chip * NB_DEV + local_blocks
    place = place * SLOT
    asked = jnp.broadcast_to(place.reshape(1, 2, 1, RQ), (4, 2, 16, RQ)).reshape(DEVICES, RQ)
    wanted = exchange(asked, ALL)

    stripes = make_stripes(node_codes, node_scales.astype(jnp.float32))
    own = exchange(stripes.reshape(CHIP_COUNT, NB_DEV, HALF), CHIPS)
    own = own.reshape(TABLE, HALF)
    sister = lax.ppermute(own, "core", SWAP)
    send = gather(wanted, own, sister)
    send, neighbours, target_rows = lax.optimization_barrier((send, neighbours, target_rows))
    got = exchange(send, ALL)

    block, row = neighbours // BR, neighbours % BR
    column = (row // 8) * 1024 + (block // RQ) * 512 + (row % 8) * RQ + block % RQ
    x_t, pre_self, tally = side(
        target_rows, column, node_codes, node_scales.astype(jnp.float32), weight_self, bias
    )
    which = core.reshape(1).astype(jnp.int32)
    hidden, kept, given = layer(
        which, got, tally, pre_self, x_t, weight_neigh, cotangent
    )
    return (hidden,) + sum_over_devices(kept, given, which)


def solution(mesh):
    fine = Mesh(mesh.devices.reshape(4, 2, 4, 4), ALL)
    placed = (
        P(ALL, None),
        P(ALL),
        P(ALL),
        P(ALL, None),
        P(ALL),
        P(ALL, None),
        P(),
        P(),
        P(),
        P(ALL, None),
    )
    return jax.shard_map(
        local,
        mesh=fine,
        in_specs=placed,
        out_specs=(P(ALL, None), P(), P(), P()),
        check_vma=False,
    )
```

```python
import jax
import jax.numpy as jnp
from jax import lax
from jax.experimental import pallas as pl
from jax.experimental.pallas import tpu as pltpu
from jax.sharding import Mesh, PartitionSpec as P

F = 768
H = 1024
BR = 32
K = 10
NODE_DEV = 2048
TGT = 1024
NB_DEV = 64
R_DEV = 128
CHIP_COUNT = 64
DEVICES = 128
HALF = F // 2
RQ = R_DEV // 2
ALL = ("z", "core", "x", "y")
CHIPS = ("z", "x", "y")
SWAP = [(0, 1), (1, 0)]
HB = 256
RB = 96
RBP = 104


def exchange(array, axes):
    return lax.all_to_all(array, axes, split_axis=0, concat_axis=0, tiled=True)


PITCH = BR + 4


def stripe_copy(codes_ref, codes, sem, k):
    lanes = pl.ds(pl.multiple_of(k * 128, 128), 128)
    return pltpu.make_async_copy(codes_ref.at[:, lanes], codes.at[k], sem.at[k])


def stripe_kernel(codes_ref, scales_ref, stripes_ref, codes, scales, wide, sem):
    k = pl.program_id(0)

    @pl.when(k == 0)
    def _():
        for n in range(6):
            stripe_copy(codes_ref, codes, sem, n).start()
        columns = scales_ref[...].T
        for c in range(NODE_DEV // 128):
            scales[c * 128 : (c + 1) * 128, :] = jnp.broadcast_to(columns[:, c : c + 1], (128, 128))

    stripe_copy(codes_ref, codes, sem, k).wait()
    product = codes[k].astype(jnp.float32) * scales[...]
    for b in range(NB_DEV):
        wide[b * PITCH : b * PITCH + BR, :] = product[b * BR : (b + 1) * BR]
    for row in range(BR):
        stripes_ref[row, 0] = wide[pl.ds(row, NB_DEV, stride=PITCH), :].astype(jnp.bfloat16)


def make_stripes(codes, scales):
    return pl.pallas_call(
        stripe_kernel,
        grid=(6,),
        in_specs=[
            pl.BlockSpec(memory_space=pl.ANY),
            pl.BlockSpec((NODE_DEV // 128, 128), lambda k: (0, 0)),
        ],
        out_specs=pl.BlockSpec((BR, 1, NB_DEV, 128), lambda k: (0, k // 3, 0, k % 3)),
        out_shape=jax.ShapeDtypeStruct((BR, 2, NB_DEV, HALF), jnp.bfloat16),
        scratch_shapes=[
            pltpu.VMEM((6, NODE_DEV, 128), jnp.bfloat16),
            pltpu.VMEM((NODE_DEV, 128), jnp.float32),
            pltpu.VMEM((NB_DEV * PITCH, 128), jnp.float32),
            pltpu.SemaphoreType.DMA((6,)),
        ],
        compiler_params=pltpu.CompilerParams(vmem_limit_bytes=60 << 20),
        name="make_stripes",
    )(codes, scales.reshape(NODE_DEV // 128, 128))


GROUP = 16
TABLE = CHIP_COUNT * NB_DEV
SLOT = 4


STAGES = 8
STAGE = 2 * TABLE // STAGES


def gather_kernel(wanted_ref, own_ref, sister_ref, out_ref, table, picked, narrow, sem):
    @pl.when(pl.program_id(0) == 0)
    def _():
        copies = []
        for n in range(STAGES):
            source = own_ref if n < STAGES // 2 else sister_ref
            start = n % (STAGES // 2) * STAGE
            copies.append(
                pltpu.make_async_copy(source.at[pl.ds(start, STAGE)], narrow.at[n], sem.at[n])
            )
            copies[-1].start()
        for n in range(STAGES):
            copies[n].wait()
            for k in range(3):
                table[pl.ds(n * STAGE * SLOT + k, STAGE, stride=SLOT), :] = narrow[
                    n, :, k * 128 : (k + 1) * 128
                ].astype(jnp.float32)

    first = pl.program_id(0) * GROUP

    def pair(step, carry):
        for u in range(2):
            base = u * RQ * SLOT
            for j in range(RQ):
                at = pl.multiple_of(wanted_ref[first + 2 * step + u, j], SLOT)
                picked[pl.ds(base + j * SLOT, SLOT), :] = table[pl.ds(at, SLOT), :]
        for u in range(2):
            base = u * RQ * SLOT
            for k in range(3):
                out_ref[2 * step + u, :, k * 128 : (k + 1) * 128] = picked[
                    pl.ds(base + k, RQ, stride=SLOT), :
                ].astype(jnp.bfloat16)
        return carry

    lax.fori_loop(0, GROUP // 2, pair, 0)


def gather(wanted, own, sister):
    return pl.pallas_call(
        gather_kernel,
        grid_spec=pltpu.PrefetchScalarGridSpec(
            num_scalar_prefetch=1,
            grid=(DEVICES // GROUP,),
            in_specs=[
                pl.BlockSpec(memory_space=pl.ANY),
                pl.BlockSpec(memory_space=pl.ANY),
            ],
            out_specs=pl.BlockSpec((GROUP, RQ, HALF), lambda i, w: (i, 0, 0)),
            scratch_shapes=[
                pltpu.VMEM((2 * TABLE * SLOT, 128), jnp.float32),
                pltpu.VMEM((2 * RQ * SLOT, 128), jnp.float32),
                pltpu.VMEM((STAGES, STAGE, HALF), jnp.bfloat16),
                pltpu.SemaphoreType.DMA((STAGES,)),
            ],
        ),
        out_shape=pltpu.HBM((DEVICES, RQ, HALF), jnp.bfloat16),
        compiler_params=pltpu.CompilerParams(vmem_limit_bytes=27 << 20),
        name="gather_rows",
    )(wanted, own, sister)


SIDE = 128


def side_kernel(
    target_ref, column_ref, codes_ref, scales_ref, weight_ref, bias_ref, x_t_ref, pre_ref, tally_ref
):
    hit = target_ref[...] == lax.broadcasted_iota(jnp.int32, (SIDE, NODE_DEV), 1)
    picker = hit.astype(jnp.float32).astype(jnp.bfloat16)
    own_codes = jnp.dot(picker, codes_ref[...], preferred_element_type=jnp.float32)
    own_scales = jnp.sum(jnp.where(hit, scales_ref[...], 0.0), axis=1, keepdims=True)
    x_self = (own_codes * own_scales).astype(jnp.bfloat16)
    x_t_ref[...] = x_self.T
    pre_ref[...] = bias_ref[...] + jnp.dot(
        x_self, weight_ref[...], preferred_element_type=jnp.float32
    )
    wide = 256

    def count(c, carry):
        first = pl.multiple_of(c * wide, wide)
        ids = lax.broadcasted_iota(jnp.int32, (SIDE, wide), 1) + first
        total = jnp.zeros((SIDE, wide), jnp.float32)
        for k in range(K):
            total = total + jnp.where(column_ref[:, k : k + 1] == ids, 1.0, 0.0)
        tally_ref[:, pl.ds(first, wide)] = total.astype(jnp.bfloat16)
        return carry

    lax.fori_loop(0, R_DEV * BR // wide, count, 0)


def side(targets, columns, codes, scales, weight, bias):
    same = lambda i: (0, 0)
    return pl.pallas_call(
        side_kernel,
        grid=(TGT // SIDE,),
        in_specs=[
            pl.BlockSpec((SIDE, 1), lambda i: (i, 0)),
            pl.BlockSpec((SIDE, K), lambda i: (i, 0)),
            pl.BlockSpec((NODE_DEV, F), same),
            pl.BlockSpec((1, NODE_DEV), same),
            pl.BlockSpec((F, H), same),
            pl.BlockSpec((1, H), same),
        ],
        out_specs=[
            pl.BlockSpec((F, SIDE), lambda i: (0, i)),
            pl.BlockSpec((SIDE, H), lambda i: (i, 0)),
            pl.BlockSpec((SIDE, R_DEV * BR), lambda i: (i, 0)),
        ],
        out_shape=[
            jax.ShapeDtypeStruct((F, TGT), jnp.bfloat16),
            jax.ShapeDtypeStruct((TGT, H), jnp.float32),
            jax.ShapeDtypeStruct((TGT, R_DEV * BR), jnp.bfloat16),
        ],
        compiler_params=pltpu.CompilerParams(vmem_limit_bytes=24 << 20),
        name="side",
    )(targets[:, None], columns, codes, scales[None, :], weight, bias[None, :])


MEAN_STEPS = 4
COLS = R_DEV * BR // MEAN_STEPS
PIECES = DEVICES // MEAN_STEPS
LATE = H // HB


def layer_kernel(
    core_ref, got_ref, tally_ref, pre_ref, x_t_ref, weight_ref, cot_ref,
    hidden_ref, kept_ref, given_ref,
    got, tally, pre_self, x_t, weight, cot, hidden, acc, mean, mean_t, sem, out_sem,
):
    count = 0

    def fetch(source, target):
        nonlocal count
        copy = pltpu.make_async_copy(source, target, sem.at[count])
        count += 1
        copy.start()
        return copy

    early = []
    for n in range(MEAN_STEPS):
        early.append(
            (
                fetch(got_ref.at[pl.ds(n * PIECES, PIECES)], got.at[n]),
                fetch(tally_ref.at[:, pl.ds(n * COLS, COLS)], tally.at[n]),
            )
        )
    late = [
        fetch(source, target)
        for source, target in (
            (weight_ref, weight), (pre_ref, pre_self), (cot_ref, cot), (x_t_ref, x_t)
        )
    ]
    for n in range(MEAN_STEPS):
        for copy in early[n]:
            copy.wait()
        rows = jnp.concatenate(
            [
                jnp.concatenate([got[n, 2 * e + half] for e in range(COLS // RQ)], axis=0)
                for half in range(2)
            ],
            axis=1,
        )
        part = jnp.dot(tally[n], rows, preferred_element_type=jnp.float32)
        if n == 0:
            acc[...] = part
        elif n < MEAN_STEPS - 1:
            acc[...] += part
        else:
            value = ((acc[...] + part) * (1.0 / K)).astype(jnp.bfloat16)
            mean[...] = value
            mean_t[...] = value.T
    for copy in late:
        copy.wait()
    first = core_ref[0] == 0
    leaving = []
    for n in range(LATE):
        block = slice(n * HB, (n + 1) * HB)
        pre = pre_self[:, block] + jnp.dot(
            mean[...], weight[:, block], preferred_element_type=jnp.float32
        )
        square = pre * pre
        tangent = jnp.tanh(pre * (0.7978845608 + (0.7978845608 * 0.044715) * square))
        rest = 0.5 + 0.5 * tangent
        hidden[:, block] = (pre * rest).astype(jnp.bfloat16)
        slope = rest + pre * (1.0 - tangent * tangent) * (
            0.5 * 0.7978845608 + (1.5 * 0.7978845608 * 0.044715) * square
        )
        delta = (cot[:, block].astype(jnp.float32) * slope).astype(jnp.bfloat16)
        bias_term = jnp.sum(delta.astype(jnp.float32), axis=0, keepdims=True)
        grad_self = jnp.dot(x_t[...], delta, preferred_element_type=jnp.float32)
        grad_neigh = jnp.dot(mean_t[...], delta, preferred_element_type=jnp.float32)
        tail = jnp.broadcast_to(bias_term, (RBP - RB, HB))
        for ref, value in (
            (given_ref, jnp.where(first, grad_neigh, grad_self)),
            (kept_ref, jnp.where(first, grad_self, grad_neigh)),
        ):
            for c in range(HB // 128):
                lanes = slice(c * 128, (c + 1) * 128)
                for r in range(8):
                    ref[r, n * (HB // 128) + c] = jnp.concatenate(
                        [value[r * RB : (r + 1) * RB, lanes], tail[:, lanes]], axis=0
                    ).astype(jnp.bfloat16)
        lanes = pl.ds(n * HB, HB)
        copy = pltpu.make_async_copy(hidden.at[:, lanes], hidden_ref.at[:, lanes], out_sem.at[n])
        copy.start()
        leaving.append(copy)
    for copy in leaving:
        copy.wait()


def layer(core, got, tally, pre_self, x_t, weight_neigh, cotangent):
    whole = pl.BlockSpec(memory_space=pl.ANY)
    return pl.pallas_call(
        layer_kernel,
        in_specs=[pl.BlockSpec(memory_space=pltpu.SMEM)] + [whole] * 6,
        out_specs=[whole] + [pl.BlockSpec(memory_space=pltpu.VMEM)] * 2,
        out_shape=[
            jax.ShapeDtypeStruct((TGT, H), jnp.bfloat16),
            pltpu.VMEM((8, 8, RBP, 128), jnp.bfloat16),
            pltpu.VMEM((8, 8, RBP, 128), jnp.bfloat16),
        ],
        scratch_shapes=[
            pltpu.VMEM((MEAN_STEPS, PIECES, RQ, HALF), jnp.bfloat16),
            pltpu.VMEM((MEAN_STEPS, TGT, COLS), jnp.bfloat16),
            pltpu.VMEM((TGT, H), jnp.float32),
            pltpu.VMEM((F, TGT), jnp.bfloat16),
            pltpu.VMEM((F, H), jnp.bfloat16),
            pltpu.VMEM((TGT, H), jnp.bfloat16),
            pltpu.VMEM((TGT, H), jnp.bfloat16),
            pltpu.VMEM((TGT, F), jnp.float32),
            pltpu.VMEM((TGT, F), jnp.bfloat16),
            pltpu.VMEM((F, TGT), jnp.bfloat16),
            pltpu.SemaphoreType.DMA((2 * MEAN_STEPS + 4,)),
            pltpu.SemaphoreType.DMA((LATE,)),
        ],
        compiler_params=pltpu.CompilerParams(vmem_limit_bytes=58 << 20),
        name="layer",
    )(core, got, tally, pre_self, x_t, weight_neigh, cotangent)


def unpack_kernel(core_ref, full_ref, theirs_ref, self_ref, neigh_ref, bias_ref):
    first = core_ref[0] == 0
    for r in range(2):
        rows = slice(r * RB, (r + 1) * RB)
        for c in range(8):
            lanes = slice(c * 128, (c + 1) * 128)
            a = full_ref[r, c].astype(jnp.float32)
            b = theirs_ref[r, c].astype(jnp.float32)
            self_ref[rows, lanes] = jnp.where(first, a[:RB], b[:RB])
            neigh_ref[rows, lanes] = jnp.where(first, b[:RB], a[:RB])
            bias_ref[:, lanes] = a[RB : RB + 1]


def unpack(core, full, theirs):
    chunks = pl.BlockSpec((2, 8, RBP, 128), lambda i, w: (i, 0, 0, 0))
    return pl.pallas_call(
        unpack_kernel,
        grid_spec=pltpu.PrefetchScalarGridSpec(
            num_scalar_prefetch=1,
            grid=(4,),
            in_specs=[chunks, chunks],
            out_specs=[
                pl.BlockSpec((2 * RB, H), lambda i, w: (i, 0)),
                pl.BlockSpec((2 * RB, H), lambda i, w: (i, 0)),
                pl.BlockSpec((1, H), lambda i, w: (0, 0)),
            ],
        ),
        out_shape=[
            jax.ShapeDtypeStruct((F, H), jnp.float32),
            jax.ShapeDtypeStruct((F, H), jnp.float32),
            jax.ShapeDtypeStruct((1, H), jnp.float32),
        ],
        compiler_params=pltpu.CompilerParams(vmem_limit_bytes=12 << 20),
        name="unpack",
    )(core, full.reshape(8, 8, RBP, 128), theirs.reshape(8, 8, RBP, 128))


def sum_over_devices(kept, given, core):
    kept = kept.reshape(CHIP_COUNT, RBP, 128)
    received = lax.ppermute(given.reshape(CHIP_COUNT, RBP, 128), "core", SWAP)
    chip = (kept.astype(jnp.float32) + received.astype(jnp.float32)).astype(jnp.bfloat16)
    parts = exchange(chip, CHIPS)
    mine = jnp.sum(parts.astype(jnp.float32), axis=0).astype(jnp.bfloat16)
    full = exchange(jnp.broadcast_to(mine[None], (CHIP_COUNT, RBP, 128)), CHIPS)
    theirs = lax.ppermute(full, "core", SWAP)
    grad_self, grad_neigh, grad_bias = unpack(core, full, theirs)
    return grad_self, grad_neigh, grad_bias.reshape(H)


def local(
    node_codes, node_scales, target_rows, owners, local_blocks, neighbours,
    weight_self, weight_neigh, bias, cotangent,
):
    core = lax.axis_index("core")
    owner = owners[:, 0]
    owner_core = (owner // 16) % 2
    owner_chip = (owner // 32) * 16 + owner % 16
    serving = (jnp.arange(R_DEV, dtype=jnp.int32) // RQ) % 2
    place = (owner_core != serving).astype(jnp.int32) * TABLE + owner_chip * NB_DEV + local_blocks
    place = place * SLOT
    asked = jnp.broadcast_to(place.reshape(1, 2, 1, RQ), (4, 2, 16, RQ)).reshape(DEVICES, RQ)
    wanted = exchange(asked, ALL)

    stripes = make_stripes(node_codes, node_scales.astype(jnp.float32))
    own = exchange(stripes.reshape(CHIP_COUNT, NB_DEV, HALF), CHIPS)
    own = own.reshape(TABLE, HALF)
    sister = lax.ppermute(own, "core", SWAP)
    send = gather(wanted, own, sister)
    send, neighbours, target_rows = lax.optimization_barrier((send, neighbours, target_rows))
    got = exchange(send, ALL)

    block, row = neighbours // BR, neighbours % BR
    column = (row // 8) * 1024 + (block // RQ) * 512 + (row % 8) * RQ + block % RQ
    x_t, pre_self, tally = side(
        target_rows, column, node_codes, node_scales.astype(jnp.float32), weight_self, bias
    )
    which = core.reshape(1).astype(jnp.int32)
    hidden, kept, given = layer(
        which, got, tally, pre_self, x_t, weight_neigh, cotangent
    )
    return (hidden,) + sum_over_devices(kept, given, which)


def solution(mesh):
    fine = Mesh(mesh.devices.reshape(4, 2, 4, 4), ALL)
    placed = (
        P(ALL, None),
        P(ALL),
        P(ALL),
        P(ALL, None),
        P(ALL),
        P(ALL, None),
        P(),
        P(),
        P(),
        P(ALL, None),
    )
    return jax.shard_map(
        local,
        mesh=fine,
        in_specs=placed,
        out_specs=(P(ALL, None), P(), P(), P()),
        check_vma=False,
    )
```
